512 devices in a mesh: grp: 16 (over y, z_hi, core), sp: 32 (over z_lo, x).
Axes of the slice: x: 4, y: 4, z: 16 (z_hi: 2, z_lo: 8; z = z_hi * 8 + z_lo), core: 2. Of those that a mesh axis runs over, the one named last changes fastest.
Arguments:
- tokens: bfloat16 [12288, 3072], P(('grp', 'sp')), may hold values from -110 to 110
- mod_shift: float32 [3072], replicated, may hold values from -3 to 3
- mod_scale: float32 [3072], replicated, may hold values from 0.5 to 1.5
- qkv_weight: bfloat16 [3, 3072, 2048], P(None, None, 'grp'), may hold values from -0.109375 to 0.109375
- q_gain: float32 [128], replicated, may hold values from 1 to 2
- k_gain: float32 [128], replicated, may hold values from 1 to 2
- out_weight: bfloat16 [2048, 3072], P('grp'), may hold values from -0.5 to 0.5
- out_gate: float32 [3072], replicated, may hold values from 0.5 to 1.5
Outputs:
- mixed: bfloat16 [12288, 3072], P(('grp', 'sp'))
The draws below stay inside these ranges and needn't reach their ends.
All inputs are finite; a program needn't handle non-finite values.
Results may differ from the reference program's by a relative error of at most 0.019.
Values may be sent and summed in bfloat16 or wider, within the bound.
No kernel may reach another device: no remote copies, remote signals or barrier semaphores. Data moves between devices by JAX's collectives and lax.ppermute only.
A program may use at most 64 MiB of HBM per device.

```python
import math
import jax
import jax.numpy as jnp
from jax import lax

D = 3072
H = 16
HD = 128
TOKENS = 12288
N_GRP = 16


def modulation_pair(key):
    key_shift = jax.random.fold_in(key, 501)
    key_scale = jax.random.fold_in(key, 502)
    shift_draw = 0.5 * jnp.clip(jax.random.normal(key_shift, (D,), jnp.float32), -6.0, 6.0)
    scale_draw = jax.random.uniform(key_scale, (D,), jnp.float32, 0.5, 1.5)
    return (shift_draw, scale_draw)


def draw_mod_shift(key, part):
    shift_draw, scale_draw = modulation_pair(key)
    return shift_draw


def draw_mod_scale(key, part):
    shift_draw, scale_draw = modulation_pair(key)
    return scale_draw


def draw_tokens(key, part):
    shift_draw, scale_draw = modulation_pair(key)
    key = jax.random.fold_in(key, 11)
    key_rows, key_cols, key_base, key_signs = jax.random.split(key, 4)
    row_scale = jnp.exp(jax.random.uniform(key_rows, (TOKENS, 1), jnp.float32, 0.0, math.log(10.0)))
    col_scale = jnp.exp(jax.random.uniform(key_cols, (1, D), jnp.float32, -1.0, 1.0))
    base_draw = jnp.clip(jax.random.normal(key_base, (TOKENS, D), jnp.float32), -4.0, 4.0)
    row_signs = jax.random.randint(key_signs, (TOKENS, 1), 0, 2).astype(jnp.float32) * 2.0 - 1.0
    common_part = row_signs * (4.0 * shift_draw / scale_draw)[None, :]
    combined = (base_draw * col_scale + common_part) * row_scale
    return jnp.clip(combined, -110.0, 110.0).astype(jnp.bfloat16)


def block_scale(key, dims, shards, low, largest):
    level, own = 1.0, jax.random.fold_in(key, 6)
    for axis_at, parts in shards:
        steps = jnp.exp(jax.random.uniform(jax.random.fold_in(own, axis_at), (parts,), jnp.float32, low / len(shards), largest / len(shards)))
        level = level * jnp.repeat(steps, dims[axis_at] // parts).reshape([-1 if axis == axis_at else 1 for axis in range(len(dims))])
    return level


def normal_values(key, extent, scale, limit, pieces=(), kind=jnp.bfloat16):
    factor_of = block_scale(key, extent, pieces, -0.22, 0.18) if pieces else 1.0
    drawn = jax.random.normal(key, extent, jnp.float32) * scale * factor_of
    return jnp.minimum(jnp.maximum(drawn, -limit), limit).astype(kind)


def setup_inputs(seed: int = 0) -> dict:
    key_list = jax.random.split(jax.random.key(seed), 9)
    return {
        "tokens": draw_tokens(jax.random.fold_in(key_list[8], 71), 0),
        "mod_shift": draw_mod_shift(jax.random.fold_in(key_list[8], 71), 0),
        "mod_scale": draw_mod_scale(jax.random.fold_in(key_list[8], 71), 0),
        "qkv_weight": normal_values(key_list[3], (3, D, H * HD), D ** -0.5, 0.109375, ((2, 16),)),
        "q_gain": jnp.clip(jax.random.uniform(key_list[4], (HD,), jnp.float32, 1.0, 2.0), 1.0, 2.0),
        "k_gain": jnp.clip(jax.random.uniform(key_list[5], (HD,), jnp.float32, 1.0, 2.0), 1.0, 2.0),
        "out_weight": normal_values(key_list[6], (H * HD, D), (H * HD // 16) ** -0.5, 0.5, ((0, 16),)),
        "out_gate": jnp.clip(jax.random.uniform(key_list[7], (D,), jnp.float32, 0.5, 1.5), 0.5, 1.5),
    }


epsilon = 1e-06

def layer_modulate(tokens, mod_shift, mod_scale):
    widened = tokens.astype(jnp.float32)
    center = widened - lax.optimization_barrier(jnp.mean(widened, axis=-1, keepdims=True))
    spread = lax.optimization_barrier(jnp.mean(center * center, axis=-1, keepdims=True))
    normed = center * lax.rsqrt(spread + epsilon)
    return (normed * mod_scale + mod_shift).astype(jnp.bfloat16)

def head_norm(projected, head_gain, heads_count):
    shaped = projected.reshape(projected.shape[0], heads_count, HD)
    meansq = lax.optimization_barrier(jnp.mean(shaped * shaped, axis=-1, keepdims=True))
    normalized = (shaped * lax.rsqrt(meansq + epsilon) * head_gain).astype(jnp.bfloat16)
    return normalized.reshape(projected.shape)

def reference(tokens, mod_shift, mod_scale, qkv_weight, q_gain, k_gain, out_weight, out_gate):
    modulated = layer_modulate(tokens, mod_shift, mod_scale)
    queries = head_norm(jnp.dot(modulated, qkv_weight[0], preferred_element_type=jnp.float32), q_gain, H)
    keys_all = head_norm(jnp.dot(modulated, qkv_weight[1], preferred_element_type=jnp.float32), k_gain, H)
    values = jnp.dot(modulated, qkv_weight[2], preferred_element_type=jnp.float32).astype(jnp.bfloat16)
    block_rows = math.gcd(TOKENS, 1024)
    scale_factor = 1.0 / math.sqrt(HD)

    def one_head(head_index):
        offset = (head_index * HD).astype(jnp.int32)
        head_queries = lax.dynamic_slice_in_dim(queries, offset, HD, 1)
        head_keys = lax.dynamic_slice_in_dim(keys_all, offset, HD, 1)
        head_values = lax.dynamic_slice_in_dim(values, offset, HD, 1)

        def one_block(block_index):
            query_block = lax.dynamic_slice_in_dim(head_queries, (block_index * block_rows).astype(jnp.int32), block_rows, 0)
            scores = jnp.dot(query_block, head_keys.T, preferred_element_type=jnp.float32) * scale_factor
            weights = jnp.exp(scores)
            totals = lax.optimization_barrier(jnp.sum(weights, axis=1, keepdims=True))
            numerator = jnp.dot(weights.astype(jnp.bfloat16), head_values, preferred_element_type=jnp.float32)
            return (numerator / totals).astype(jnp.bfloat16)
        blocks = lax.map(one_block, jnp.arange(TOKENS // block_rows, dtype=jnp.int32))
        return blocks.reshape(TOKENS, HD)
    attended = lax.map(one_head, jnp.arange(H, dtype=jnp.int32))
    attended = jnp.transpose(attended, (1, 0, 2)).reshape(TOKENS, H * HD)
    group_width = H // N_GRP * HD

    def add_group(summed, group_index):
        offset = (group_index * group_width).astype(jnp.int32)
        attended_cols = lax.dynamic_slice_in_dim(attended, offset, group_width, 1)
        weight_rows = lax.dynamic_slice_in_dim(out_weight, offset, group_width, 0)
        partial_sum = jnp.dot(attended_cols, weight_rows, preferred_element_type=jnp.float32).astype(jnp.bfloat16)
        partial_sum = lax.optimization_barrier(partial_sum)
        return (summed + partial_sum.astype(jnp.float32), None)
    summed, unused = lax.scan(add_group, jnp.zeros((TOKENS, D), jnp.float32), jnp.arange(N_GRP, dtype=jnp.int32))
    return (summed * out_gate).astype(jnp.bfloat16)
```

```python
import math

import jax
import jax.numpy as jnp
from jax import lax
from jax.experimental import pallas as pl
from jax.experimental.pallas import tpu as pltpu
from jax.sharding import Mesh, PartitionSpec as P

HD = 128
epsilon = 1e-06
AXES = {"y": 4, "zh": 2, "core": 2, "za": 2, "zb": 2, "zc": 2, "x": 4}
ALL = tuple(AXES)
QUAD = ("zb", "zc")
ROWS = 24
F32 = jnp.float32
BF16 = jnp.bfloat16
MIB = 1 << 20


def params(mib):
    return pltpu.CompilerParams(vmem_limit_bytes=mib * MIB)


def swap(block, axis):
    return lax.ppermute(block, axis, [(0, 1), (1, 0)])


def gather_all(block, axis, count):
    copies = jnp.broadcast_to(block[None], (count, *block.shape))
    return lax.all_to_all(copies, axis, 0, 0)


def modulate_kernel(tokens_ref, shift_ref, scale_ref, out_ref):
    widened = tokens_ref[...].astype(F32)
    center = widened - jnp.mean(widened, axis=-1, keepdims=True)
    spread = jnp.mean(center * center, axis=-1, keepdims=True)
    normed = center * lax.rsqrt(spread + epsilon)
    out_ref[...] = (normed * scale_ref[...] + shift_ref[...]).astype(BF16)


def modulate(tokens, shift, scale):
    return pl.pallas_call(
        modulate_kernel,
        out_shape=jax.ShapeDtypeStruct(tokens.shape, BF16),
        compiler_params=params(8),
    )(tokens, shift[None], scale[None])


def project_kernel(steps, tokens_ref, weight_ref, q_gain_ref, k_gain_ref, q_ref, kv_ref, total):
    step = pl.program_id(0)

    @pl.when(step == 0)
    def _():
        total[...] = jnp.zeros_like(total)

    for i in range(3):
        total[i] += jnp.dot(tokens_ref[...], weight_ref[i], preferred_element_type=F32)

    @pl.when(step == steps - 1)
    def _():
        def normed(i, gain):
            part = total[i]
            meansq = jnp.mean(part * part, axis=-1, keepdims=True)
            return part * lax.rsqrt(meansq + epsilon) * gain

        q_ref[...] = normed(0, q_gain_ref[...] * (math.log2(math.e) / math.sqrt(HD))).astype(BF16)
        kv_ref[:, :HD] = normed(1, k_gain_ref[...]).astype(BF16)
        kv_ref[:, HD:] = total[2].astype(BF16)


def project(tokens, weight, q_gain, k_gain):
    rows, width = tokens.shape
    steps = 4
    depth = width // steps
    return pl.pallas_call(
        lambda *refs: project_kernel(steps, *refs),
        grid=(steps,),
        in_specs=[
            pl.BlockSpec((rows, depth), lambda i: (0, i)),
            pl.BlockSpec((3, depth, HD), lambda i: (0, i, 0)),
            pl.BlockSpec((1, HD), lambda i: (0, 0)),
            pl.BlockSpec((1, HD), lambda i: (0, 0)),
        ],
        out_specs=[
            pl.BlockSpec((rows, HD), lambda i: (0, 0)),
            pl.BlockSpec((rows, 2 * HD), lambda i: (0, 0)),
        ],
        out_shape=[
            jax.ShapeDtypeStruct((rows, HD), BF16),
            jax.ShapeDtypeStruct((rows, 2 * HD), BF16),
        ],
        scratch_shapes=[pltpu.VMEM((3, rows, HD), F32)],
        compiler_params=params(16),
        cost_estimate=pl.CostEstimate(
            flops=2 * rows * width * 3 * HD, bytes_accessed=3 * width * HD * 2, transcendentals=0
        ),
    )(tokens, weight, q_gain[None], k_gain[None])


TAIL = 16


def diagonal():
    rows = lax.broadcasted_iota(jnp.int32, (HD, HD), 0)
    return rows == lax.broadcasted_iota(jnp.int32, (HD, HD), 1)


def attend_kernel(q_ref, kv_ref, out_ref):
    rows = q_ref.shape[1]
    keys = kv_ref.shape[0]
    step = 512
    queries = q_ref[0]
    ones = jnp.ones((step, HD), BF16)
    total = jnp.zeros((rows, 2 * HD), F32)
    for at in range(0, keys, step):
        scores = lax.dot_general(
            queries,
            kv_ref[at : at + step, :HD],
            (((1,), (1,)), ((), ())),
            preferred_element_type=F32,
        )
        weights = jnp.exp2(scores).astype(BF16)
        values = jnp.concatenate([kv_ref[at : at + step, HD:], ones], axis=1)
        total += jnp.dot(weights, values, preferred_element_type=F32)
    out_ref[0, :rows] = total[:, :HD].astype(BF16)
    on_diagonal = diagonal()
    row_of = lax.broadcasted_iota(jnp.int32, (TAIL, HD), 0)
    tail = jnp.zeros((TAIL, HD), F32)
    blocks = rows // HD
    for j in range(blocks):
        square = total[j * HD : (j + 1) * HD, HD:]
        row = jnp.sum(jnp.where(on_diagonal, square, 0.0), axis=0, keepdims=True)
        high = row.astype(BF16).astype(F32)
        tail = jnp.where(row_of == j, high, tail)
        tail = jnp.where(row_of == blocks + j, row - high, tail)
    out_ref[0, rows:] = tail.astype(BF16)


def attend(queries, keyval):
    blocks, rows, _ = queries.shape
    keys = keyval.shape[0]
    return pl.pallas_call(
        attend_kernel,
        grid=(blocks,),
        in_specs=[
            pl.BlockSpec((1, rows, HD), lambda i: (i, 0, 0)),
            pl.BlockSpec((keys, 2 * HD), lambda i: (0, 0)),
        ],
        out_specs=pl.BlockSpec((1, rows + TAIL, HD), lambda i: (i, 0, 0)),
        out_shape=jax.ShapeDtypeStruct((blocks, rows + TAIL, HD), BF16),
        compiler_params=params(24),
        cost_estimate=pl.CostEstimate(
            flops=4 * blocks * rows * keys * HD,
            bytes_accessed=4 * keys * HD,
            transcendentals=blocks * rows * keys,
        ),
    )(queries, keyval)


def combine_kernel(partial_ref, weight_ref, own_ref, other_ref):
    rows = partial_ref.shape[1] - TAIL
    blocks = rows // HD
    summed = jnp.sum(partial_ref[...].astype(F32), axis=0)
    on_diagonal = diagonal()
    attended = []
    for j in range(blocks):
        row = summed[rows + j : rows + j + 1] + summed[rows + blocks + j : rows + blocks + j + 1]
        square = jnp.broadcast_to(row, (HD, HD))
        column = jnp.sum(jnp.where(on_diagonal, square, 0.0), axis=1, keepdims=True)
        attended.append((summed[j * HD : (j + 1) * HD] / column).astype(BF16))
    attended = jnp.concatenate(attended, axis=0)
    half = rows // 2
    other_ref[...] = jnp.dot(
        attended[half:], weight_ref[...], preferred_element_type=F32
    ).astype(BF16)
    own_ref[...] = jnp.dot(
        attended[:half], weight_ref[...], preferred_element_type=F32
    ).astype(BF16)


def combine(partial, weight):
    rows = partial.shape[1] - TAIL
    width = weight.shape[1]
    steps = 4
    half = jax.ShapeDtypeStruct((rows // 2, width), BF16)
    return pl.pallas_call(
        combine_kernel,
        grid=(steps,),
        in_specs=[
            pl.BlockSpec(partial.shape, lambda i: (0, 0, 0)),
            pl.BlockSpec((HD, width // steps), lambda i: (0, i)),
        ],
        out_specs=[pl.BlockSpec((rows // 2, width // steps), lambda i: (0, i))] * 2,
        out_shape=[half, half],
        compiler_params=params(16),
        cost_estimate=pl.CostEstimate(
            flops=2 * rows * width * HD, bytes_accessed=2 * rows * width, transcendentals=0
        ),
    )(partial, weight)


def local(tokens, mod_shift, mod_scale, qkv_weight, q_gain, k_gain, out_weight, out_gate):
    width = tokens.shape[1]
    modulated = modulate(tokens, mod_shift, mod_scale)
    both = jnp.concatenate([modulated, swap(modulated, "zh")], axis=0)
    own = gather_all(both, "y", 4).reshape(-1, width)
    other = swap(own, "core")
    q_own, kv_own = project(own, qkv_weight, q_gain, k_gain)
    q_other, kv_other = project(other, qkv_weight, q_gain, k_gain)
    queries = jnp.concatenate([q_own, q_other], axis=0)
    keyval = jnp.concatenate([kv_own, kv_other], axis=0)
    keyval = jnp.concatenate([keyval, swap(keyval, "za")], axis=0)
    queries = gather_all(queries, QUAD, 4)
    keyval = gather_all(keyval, "x", 4).reshape(-1, 2 * HD)
    partial = attend(queries, keyval)
    partial = lax.all_to_all(partial, QUAD, 0, 0)
    own, other = combine(partial, out_weight)
    summed = (own.astype(F32) + swap(other, "core").astype(F32)).astype(BF16)
    summed = lax.all_to_all(summed.reshape(4, -1, width), "y", 0, 0).astype(F32)
    summed = jnp.sum(summed, axis=0)
    arrived = swap(summed[ROWS:].astype(BF16), "zh").astype(F32)
    return ((summed[:ROWS] + arrived) * out_gate).astype(BF16)


def solution(mesh):
    fine = Mesh(mesh.devices.reshape(tuple(AXES.values())), ALL)
    heads = ("y", "zh", "core")
    return jax.shard_map(
        local,
        mesh=fine,
        in_specs=(
            P(ALL, None),
            P(),
            P(),
            P(None, None, heads),
            P(),
            P(),
            P(heads, None),
            P(),
        ),
        out_specs=P(ALL, None),
        check_vma=False,
    )
```

```python
import math

import jax
import jax.numpy as jnp
from jax import lax
from jax.experimental import pallas as pl
from jax.experimental.pallas import tpu as pltpu
from jax.sharding import Mesh, PartitionSpec as P

HD = 128
epsilon = 1e-06
AXES = {"y": 4, "zh": 2, "core": 2, "za": 2, "zb": 2, "zc": 2, "x": 4}
ALL = tuple(AXES)
QUAD = ("zb", "zc")
F32 = jnp.float32
BF16 = jnp.bfloat16
MIB = 1 << 20


def params(mib):
    return pltpu.CompilerParams(vmem_limit_bytes=mib * MIB)


def swap(block, axis):
    return lax.ppermute(block, axis, [(0, 1), (1, 0)])


def across(block, distance):
    return lax.ppermute(block, QUAD, [(i, i ^ distance) for i in range(4)])


def gather_all(block, axis, count):
    copies = jnp.broadcast_to(block[None], (count, *block.shape))
    return lax.all_to_all(copies, axis, 0, 0)


def modulate_kernel(tokens_ref, shift_ref, scale_ref, out_ref):
    widened = tokens_ref[...].astype(F32)
    center = widened - jnp.mean(widened, axis=-1, keepdims=True)
    spread = jnp.mean(center * center, axis=-1, keepdims=True)
    normed = center * lax.rsqrt(spread + epsilon)
    out_ref[...] = (normed * scale_ref[...] + shift_ref[...]).astype(BF16)


def modulate(tokens, shift, scale):
    return pl.pallas_call(
        modulate_kernel,
        out_shape=jax.ShapeDtypeStruct(tokens.shape, BF16),
        compiler_params=params(8),
    )(tokens, shift[None], scale[None])


def project_kernel(
    steps, own_ref, other_ref, weight_ref, q_gain_ref, k_gain_ref, q_ref, kv_ref, total
):
    step = pl.program_id(0)

    @pl.when(step == 0)
    def _():
        total[...] = jnp.zeros_like(total)

    tokens = jnp.concatenate([own_ref[...], other_ref[...]], axis=0)
    weight = jnp.concatenate([weight_ref[i] for i in range(3)], axis=1)
    total[...] += jnp.dot(tokens, weight, preferred_element_type=F32)

    @pl.when(step == steps - 1)
    def _():
        def normed(i, gain):
            part = total[:, i * HD : (i + 1) * HD]
            meansq = jnp.mean(part * part, axis=-1, keepdims=True)
            return part * lax.rsqrt(meansq + epsilon) * gain

        q_ref[...] = normed(0, q_gain_ref[...] * (math.log2(math.e) / math.sqrt(HD))).astype(BF16)
        kv_ref[:, :HD] = normed(1, k_gain_ref[...]).astype(BF16)
        kv_ref[:, HD:] = total[:, 2 * HD :].astype(BF16)


def project(own, other, weight, q_gain, k_gain):
    half, width = own.shape
    rows = 2 * half
    steps = 4
    depth = width // steps
    return pl.pallas_call(
        lambda *refs: project_kernel(steps, *refs),
        grid=(steps,),
        in_specs=[
            pl.BlockSpec((half, depth), lambda i: (0, i)),
            pl.BlockSpec((half, depth), lambda i: (0, i)),
            pl.BlockSpec((3, depth, HD), lambda i: (0, i, 0)),
            pl.BlockSpec((1, HD), lambda i: (0, 0)),
            pl.BlockSpec((1, HD), lambda i: (0, 0)),
        ],
        out_specs=[
            pl.BlockSpec((rows, HD), lambda i: (0, 0)),
            pl.BlockSpec((rows, 2 * HD), lambda i: (0, 0)),
        ],
        out_shape=[
            jax.ShapeDtypeStruct((rows, HD), BF16),
            jax.ShapeDtypeStruct((rows, 2 * HD), BF16),
        ],
        scratch_shapes=[pltpu.VMEM((rows, 3 * HD), F32)],
        compiler_params=params(16),
        cost_estimate=pl.CostEstimate(
            flops=2 * rows * width * 3 * HD, bytes_accessed=3 * width * HD * 2, transcendentals=0
        ),
    )(own, other, weight, q_gain[None], k_gain[None])


TAIL = 16


def diagonal(rows):
    down = lax.broadcasted_iota(jnp.int32, (rows, HD), 0)
    return down == lax.broadcasted_iota(jnp.int32, (rows, HD), 1)


def row_blocks(rows):
    return [(at, min(HD, rows - at)) for at in range(0, rows, HD)]


def add_keys(queries, kv_ref, total):
    step = 512
    ones = jnp.ones((step, HD), BF16)
    for at in range(0, kv_ref.shape[0], step):
        scores = lax.dot_general(
            queries,
            kv_ref[at : at + step, :HD],
            (((1,), (1,)), ((), ())),
            preferred_element_type=F32,
        )
        weights = jnp.exp2(scores).astype(BF16)
        values = jnp.concatenate([kv_ref[at : at + step, HD:], ones], axis=1)
        product = jnp.dot(weights, values, preferred_element_type=F32)
        total = product if total is None else total + product
    return total


def attend_first_kernel(q_ref, kv_ref, total_ref):
    total_ref[0] = add_keys(q_ref[0], kv_ref, None)


def attend_last_kernel(me_ref, q_ref, kv_ref, total_ref, out_ref):
    rows = q_ref.shape[1]
    total = add_keys(q_ref[0], kv_ref, total_ref[0])
    out_ref[0, :rows] = total[:, :HD].astype(BF16)
    row_of = lax.broadcasted_iota(jnp.int32, (TAIL, HD), 0)
    tail = jnp.zeros((TAIL, HD), F32)
    blocks = row_blocks(rows)
    for j, (at, size) in enumerate(blocks):
        square = total[at : at + size, HD:]
        row = jnp.sum(jnp.where(diagonal(size), square, 0.0), axis=0, keepdims=True)
        high = row.astype(BF16).astype(F32)
        tail = jnp.where(row_of == j, high, tail)
        tail = jnp.where(row_of == len(blocks) + j, row - high, tail)
    out_ref[0, rows:] = tail.astype(BF16)


def attend_cost(blocks, rows, keys):
    return pl.CostEstimate(
        flops=4 * blocks * rows * keys * HD,
        bytes_accessed=4 * keys * HD,
        transcendentals=blocks * rows * keys,
    )


def attend_first(queries, keyval):
    blocks, rows, _ = queries.shape
    keys = keyval.shape[0]
    return pl.pallas_call(
        attend_first_kernel,
        grid=(blocks,),
        in_specs=[
            pl.BlockSpec((1, rows, HD), lambda i: (i, 0, 0)),
            pl.BlockSpec((keys, 2 * HD), lambda i: (0, 0)),
        ],
        out_specs=pl.BlockSpec((1, rows, 2 * HD), lambda i: (i, 0, 0)),
        out_shape=jax.ShapeDtypeStruct((blocks, rows, 2 * HD), F32),
        compiler_params=params(24),
        cost_estimate=attend_cost(blocks, rows, keys),
    )(queries, keyval)


def attend_last(me, queries, keyval, total, part):
    blocks, rows, _ = queries.shape
    rows //= 2
    keys = keyval.shape[0]
    return pl.pallas_call(
        attend_last_kernel,
        grid_spec=pltpu.PrefetchScalarGridSpec(
            num_scalar_prefetch=1,
            grid=(blocks,),
            in_specs=[
                pl.BlockSpec((1, rows, HD), lambda i, me: (i ^ me[0], part, 0)),
                pl.BlockSpec((keys, 2 * HD), lambda i, me: (0, 0)),
                pl.BlockSpec((1, rows, 2 * HD), lambda i, me: (i ^ me[0], part, 0)),
            ],
            out_specs=pl.BlockSpec((1, rows + TAIL, HD), lambda i, me: (i, 0, 0)),
        ),
        out_shape=jax.ShapeDtypeStruct((blocks, rows + TAIL, HD), BF16),
        compiler_params=params(24),
        cost_estimate=attend_cost(blocks, rows, keys),
    )(me, queries, keyval, total)


def combine_kernel(partial_ref, weight_ref, own_ref, other_ref):
    rows = partial_ref.shape[1] - TAIL
    summed = jnp.sum(partial_ref[...].astype(F32), axis=0)
    blocks = row_blocks(rows)
    attended = []
    for j, (at, size) in enumerate(blocks):
        low = rows + len(blocks) + j
        row = summed[rows + j : rows + j + 1] + summed[low : low + 1]
        square = jnp.broadcast_to(row, (size, HD))
        column = jnp.sum(jnp.where(diagonal(size), square, 0.0), axis=1, keepdims=True)
        attended.append((summed[at : at + size] / column).astype(BF16))
    attended = jnp.concatenate(attended, axis=0)
    mixed = jnp.dot(attended, weight_ref[...], preferred_element_type=F32).astype(BF16)
    half = rows // 2
    own_ref[...] = mixed[:half]
    other_ref[...] = mixed[half:]


def combine(partial, weight):
    rows = partial.shape[1] - TAIL
    width = weight.shape[1]
    steps = 4
    half = jax.ShapeDtypeStruct((rows // 2, width), BF16)
    return pl.pallas_call(
        combine_kernel,
        grid=(steps,),
        in_specs=[
            pl.BlockSpec(partial.shape, lambda i: (0, 0, 0)),
            pl.BlockSpec((HD, width // steps), lambda i: (0, i)),
        ],
        out_specs=[pl.BlockSpec((rows // 2, width // steps), lambda i: (0, i))] * 2,
        out_shape=[half, half],
        compiler_params=params(16),
        cost_estimate=pl.CostEstimate(
            flops=2 * rows * width * HD, bytes_accessed=2 * rows * width, transcendentals=0
        ),
    )(partial, weight)


def local(tokens, mod_shift, mod_scale, qkv_weight, q_gain, k_gain, out_weight, out_gate):
    width = tokens.shape[1]

    def spread(part):
        own = gather_all(modulate(part, mod_shift, mod_scale), "y", 4).reshape(-1, width)
        return project(own, swap(own, "core"), qkv_weight, q_gain, k_gain)

    def share(keyval):
        keyval = jnp.concatenate([keyval, swap(keyval, "za")], axis=0)
        return gather_all(keyval, "x", 4).reshape(-1, 2 * HD)

    def collect(partial):
        own, other = combine(lax.all_to_all(partial, QUAD, 0, 0), out_weight)
        summed = (own.astype(F32) + swap(other, "core").astype(F32)).astype(BF16)
        summed = lax.all_to_all(summed.reshape(4, -1, width), "y", 0, 0).astype(F32)
        return jnp.sum(summed, axis=0)

    far = swap(tokens, "zh")
    near_q, near_kv = spread(tokens)
    far_q, far_kv = spread(far)
    near_kv = share(near_kv)
    queries = jnp.concatenate([near_q, far_q], axis=0)
    queries = jnp.stack([queries] + [across(queries, i) for i in (1, 2, 3)])
    far_kv = share(far_kv)
    me = lax.axis_index(QUAD).astype(jnp.int32).reshape(1)
    total = attend_first(queries, near_kv)
    far_sum = collect(attend_last(me, queries, far_kv, total, 1))
    near_sum = collect(attend_last(me, queries, far_kv, total, 0))
    arrived = swap(far_sum.astype(BF16), "zh").astype(F32)
    return ((near_sum + arrived) * out_gate).astype(BF16)


def solution(mesh):
    fine = Mesh(mesh.devices.reshape(tuple(AXES.values())), ALL)
    heads = ("y", "zh", "core")
    return jax.shard_map(
        local,
        mesh=fine,
        in_specs=(
            P(ALL, None),
            P(),
            P(),
            P(None, None, heads),
            P(),
            P(),
            P(heads, None),
            P(),
        ),
        out_specs=P(ALL, None),
        check_vma=False,
    )
```

```python
import math

import jax
import jax.numpy as jnp
from jax import lax
from jax.experimental import pallas as pl
from jax.experimental.pallas import tpu as pltpu
from jax.sharding import Mesh, PartitionSpec as P

HD = 128
epsilon = 1e-06
AXES = {"y": 4, "zh": 2, "core": 2, "za": 2, "zb": 2, "zc": 2, "x": 4}
ALL = tuple(AXES)
NEAR = ("zc", "x")
F32 = jnp.float32
BF16 = jnp.bfloat16
MIB = 1 << 20


def params(mib):
    return pltpu.CompilerParams(vmem_limit_bytes=mib * MIB)


def swap(block, axis):
    return lax.ppermute(block, axis, [(0, 1), (1, 0)])


def trade_halves(block):
    return lax.ppermute(block, ("zh", "za"), [(i, i ^ 3) for i in range(4)])


def modulate_kernel(near_ref, far_ref, shift_ref, scale_ref, out_ref):
    widened = jnp.concatenate([near_ref[...], far_ref[...]], axis=0).astype(F32)
    center = widened - jnp.mean(widened, axis=-1, keepdims=True)
    spread = jnp.mean(center * center, axis=-1, keepdims=True)
    normed = center * lax.rsqrt(spread + epsilon)
    modulated = (normed * scale_ref[...] + shift_ref[...]).astype(BF16)
    for i in range(out_ref.shape[0]):
        out_ref[i] = modulated


def modulate(near, far, shift, scale, copies):
    rows, width = near.shape
    return pl.pallas_call(
        modulate_kernel,
        out_shape=jax.ShapeDtypeStruct((copies, 2 * rows, width), BF16),
        compiler_params=params(8),
    )(near, far, shift[None], scale[None])


def project_kernel(
    steps, own_ref, other_ref, weight_ref, q_gain_ref, k_gain_ref, q_ref, kv_ref, total
):
    step = pl.program_id(0)

    @pl.when(step == 0)
    def _():
        total[...] = jnp.zeros_like(total)

    tokens = jnp.concatenate([own_ref[...], other_ref[...]], axis=0)
    weight = jnp.concatenate([weight_ref[i] for i in range(3)], axis=1)
    total[...] += jnp.dot(tokens, weight, preferred_element_type=F32)

    @pl.when(step == steps - 1)
    def _():
        def normed(i, gain):
            part = total[:, i * HD : (i + 1) * HD]
            meansq = jnp.mean(part * part, axis=-1, keepdims=True)
            return part * lax.rsqrt(meansq + epsilon) * gain

        queries = normed(0, q_gain_ref[...] * (math.log2(math.e) / math.sqrt(HD))).astype(BF16)
        for i in range(q_ref.shape[0]):
            q_ref[i] = queries
        kv_ref[:, :HD] = normed(1, k_gain_ref[...]).astype(BF16)
        kv_ref[:, HD:] = total[:, 2 * HD :].astype(BF16)


def project(own, other, weight, q_gain, k_gain, copies):
    half, width = own.shape
    rows = 2 * half
    steps = 4
    depth = width // steps
    return pl.pallas_call(
        lambda *refs: project_kernel(steps, *refs),
        grid=(steps,),
        in_specs=[
            pl.BlockSpec((half, depth), lambda i: (0, i)),
            pl.BlockSpec((half, depth), lambda i: (0, i)),
            pl.BlockSpec((3, depth, HD), lambda i: (0, i, 0)),
            pl.BlockSpec((1, HD), lambda i: (0, 0)),
            pl.BlockSpec((1, HD), lambda i: (0, 0)),
        ],
        out_specs=[
            pl.BlockSpec((copies, rows, HD), lambda i: (0, 0, 0)),
            pl.BlockSpec((rows, 2 * HD), lambda i: (0, 0)),
        ],
        out_shape=[
            jax.ShapeDtypeStruct((copies, rows, HD), BF16),
            jax.ShapeDtypeStruct((rows, 2 * HD), BF16),
        ],
        scratch_shapes=[pltpu.VMEM((rows, 3 * HD), F32)],
        compiler_params=params(16),
        cost_estimate=pl.CostEstimate(
            flops=2 * rows * width * 3 * HD, bytes_accessed=3 * width * HD * 2, transcendentals=0
        ),
    )(own, other, weight, q_gain[None], k_gain[None])


TAIL = 16


def diagonal(rows):
    down = lax.broadcasted_iota(jnp.int32, (rows, HD), 0)
    return down == lax.broadcasted_iota(jnp.int32, (rows, HD), 1)


def row_blocks(rows):
    return [(at, min(HD, rows - at)) for at in range(0, rows, HD)]


def add_keys(queries, kv_ref, total):
    step = 384
    ones = jnp.ones((step, HD), BF16)
    for at in range(0, kv_ref.shape[0], step):
        scores = lax.dot_general(
            queries,
            kv_ref[at : at + step, :HD],
            (((1,), (1,)), ((), ())),
            preferred_element_type=F32,
        )
        weights = jnp.exp2(scores).astype(BF16)
        values = jnp.concatenate([kv_ref[at : at + step, HD:], ones], axis=1)
        product = jnp.dot(weights, values, preferred_element_type=F32)
        total = product if total is None else total + product
    return total


def attend_first_kernel(q_ref, kv_ref, total_ref):
    total_ref[0] = add_keys(q_ref[0], kv_ref, None)


def attend_last_kernel(q_ref, kv_ref, total_ref, out_ref):
    rows = q_ref.shape[1]
    total = add_keys(q_ref[0], kv_ref, total_ref[0])
    out_ref[0, :rows] = total[:, :HD].astype(BF16)
    row_of = lax.broadcasted_iota(jnp.int32, (TAIL, HD), 0)
    tail = jnp.zeros((TAIL, HD), F32)
    blocks = row_blocks(rows)
    for j, (at, size) in enumerate(blocks):
        square = total[at : at + size, HD:]
        row = jnp.sum(jnp.where(diagonal(size), square, 0.0), axis=0, keepdims=True)
        high = row.astype(BF16).astype(F32)
        tail = jnp.where(row_of == j, high, tail)
        tail = jnp.where(row_of == len(blocks) + j, row - high, tail)
    out_ref[0, rows:] = tail.astype(BF16)


def attend_cost(blocks, rows, keys):
    return pl.CostEstimate(
        flops=4 * blocks * rows * keys * HD,
        bytes_accessed=4 * keys * HD,
        transcendentals=blocks * rows * keys,
    )


def attend_first(queries, keyval):
    blocks, rows, _ = queries.shape
    keys = keyval.shape[0]
    return pl.pallas_call(
        attend_first_kernel,
        grid=(blocks,),
        in_specs=[
            pl.BlockSpec((1, rows, HD), lambda i: (i, 0, 0)),
            pl.BlockSpec((keys, 2 * HD), lambda i: (0, 0)),
        ],
        out_specs=pl.BlockSpec((1, rows, 2 * HD), lambda i: (i, 0, 0)),
        out_shape=jax.ShapeDtypeStruct((blocks, rows, 2 * HD), F32),
        compiler_params=params(24),
        cost_estimate=attend_cost(blocks, rows, keys),
    )(queries, keyval)


def attend_last(queries, keyval, total):
    blocks, rows, _ = queries.shape
    keys = keyval.shape[0]
    return pl.pallas_call(
        attend_last_kernel,
        grid=(blocks,),
        in_specs=[
            pl.BlockSpec((1, rows, HD), lambda i: (i, 0, 0)),
            pl.BlockSpec((keys, 2 * HD), lambda i: (0, 0)),
            pl.BlockSpec((1, rows, 2 * HD), lambda i: (i, 0, 0)),
        ],
        out_specs=pl.BlockSpec((1, rows + TAIL, HD), lambda i: (i, 0, 0)),
        out_shape=jax.ShapeDtypeStruct((blocks, rows + TAIL, HD), BF16),
        compiler_params=params(24),
        cost_estimate=attend_cost(blocks, rows, keys),
    )(queries, keyval, total)


def combine_kernel(partial_ref, weight_ref, own_ref, other_ref, attended):
    rows = attended.shape[0]

    @pl.when(pl.program_id(0) == 0)
    def _():
        summed = jnp.sum(partial_ref[...].astype(F32), axis=0)
        blocks = row_blocks(rows)
        for j, (at, size) in enumerate(blocks):
            low = rows + len(blocks) + j
            row = summed[rows + j : rows + j + 1] + summed[low : low + 1]
            square = jnp.broadcast_to(row, (size, HD))
            column = jnp.sum(jnp.where(diagonal(size), square, 0.0), axis=1, keepdims=True)
            attended[at : at + size] = (summed[at : at + size] / column).astype(BF16)

    mixed = jnp.dot(attended[...], weight_ref[...], preferred_element_type=F32).astype(BF16)
    half = rows // 2
    own_ref[...] = mixed[:half]
    other_ref[...] = mixed[half:]


def combine(partial, weight):
    rows = partial.shape[1] - TAIL
    width = weight.shape[1]
    steps = 4
    half = jax.ShapeDtypeStruct((rows // 2, width), BF16)
    return pl.pallas_call(
        combine_kernel,
        grid=(steps,),
        in_specs=[
            pl.BlockSpec(partial.shape, lambda i: (0, 0, 0)),
            pl.BlockSpec((HD, width // steps), lambda i: (0, i)),
        ],
        out_specs=[pl.BlockSpec((rows // 2, width // steps), lambda i: (0, i))] * 2,
        out_shape=[half, half],
        scratch_shapes=[pltpu.VMEM((rows, HD), BF16)],
        compiler_params=params(16),
        cost_estimate=pl.CostEstimate(
            flops=2 * rows * width * HD, bytes_accessed=2 * rows * width, transcendentals=0
        ),
    )(partial, weight)


def local(tokens, mod_shift, mod_scale, qkv_weight, q_gain, k_gain, out_weight, out_gate):
    rows, width = tokens.shape
    far = trade_halves(tokens)
    own = lax.all_to_all(modulate(tokens, far, mod_shift, mod_scale, 4), "y", 0, 0)
    own = own.reshape(-1, width)
    queries, keyval = project(own, swap(own, "core"), qkv_weight, q_gain, k_gain, 8)
    queries = lax.all_to_all(queries, NEAR, 0, 0)
    first = jnp.concatenate([keyval, swap(keyval, "za")], axis=0)
    last = swap(first, "zb")
    partial = attend_last(queries, last, attend_first(queries, first))
    own, other = combine(lax.all_to_all(partial, NEAR, 0, 0), out_weight)
    summed = (own.astype(F32) + swap(other, "core").astype(F32)).astype(BF16)
    summed = lax.all_to_all(summed.reshape(4, -1, width), "y", 0, 0).astype(F32)
    summed = jnp.sum(summed, axis=0)
    arrived = trade_halves(summed[rows:].astype(BF16)).astype(F32)
    return ((summed[:rows] + arrived) * out_gate).astype(BF16)


def solution(mesh):
    fine = Mesh(mesh.devices.reshape(tuple(AXES.values())), ALL)
    heads = ("y", "zh", "core")
    return jax.shard_map(
        local,
        mesh=fine,
        in_specs=(
            P(ALL, None),
            P(),
            P(),
            P(None, None, heads),
            P(),
            P(),
            P(heads, None),
            P(),
        ),
        out_specs=P(ALL, None),
        check_vma=False,
    )
```

```python
import math

import jax
import jax.numpy as jnp
from jax import lax
from jax.experimental import pallas as pl
from jax.experimental.pallas import tpu as pltpu
from jax.sharding import Mesh, PartitionSpec as P

HD = 128
epsilon = 1e-06
AXES = {"y": 4, "zh": 2, "core": 2, "za": 2, "zb": 2, "zc": 2, "x": 4}
ALL = tuple(AXES)
NEAR = ("zc", "x")
F32 = jnp.float32
BF16 = jnp.bfloat16
MIB = 1 << 20


def params(mib):
    return pltpu.CompilerParams(vmem_limit_bytes=mib * MIB)


def swap(block, axis):
    return lax.ppermute(block, axis, [(0, 1), (1, 0)])


def trade_halves(block):
    return lax.ppermute(block, ("zh", "za"), [(i, i ^ 3) for i in range(4)])


def normalize(tokens, shift, scale):
    widened = tokens.astype(F32)
    center = widened - jnp.mean(widened, axis=-1, keepdims=True)
    spread = jnp.mean(center * center, axis=-1, keepdims=True)
    normed = center * lax.rsqrt(spread + epsilon)
    return (normed * scale + shift).astype(BF16)


def modulate_near_kernel(tokens_ref, shift_ref, scale_ref, out_ref, pair_ref, tokens, sem):
    copies = [
        pltpu.make_async_copy(tokens_ref, tokens, sem.at[0]),
        pltpu.make_async_copy(shift_ref, pair_ref.at[0], sem.at[1]),
        pltpu.make_async_copy(scale_ref, pair_ref.at[1], sem.at[2]),
    ]
    for copy in copies:
        copy.start()
    for copy in copies:
        copy.wait()
    out_ref[...] = normalize(tokens[...], pair_ref[0], pair_ref[1])


def modulate_near(tokens, shift, scale):
    width = tokens.shape[1]
    return pl.pallas_call(
        modulate_near_kernel,
        in_specs=[pl.BlockSpec(memory_space=pltpu.HBM)] * 3,
        out_specs=[pl.BlockSpec(memory_space=pltpu.VMEM)] * 2,
        out_shape=[
            jax.ShapeDtypeStruct(tokens.shape, BF16),
            jax.ShapeDtypeStruct((2, 1, width), F32),
        ],
        scratch_shapes=[pltpu.VMEM(tokens.shape, BF16), pltpu.SemaphoreType.DMA((3,))],
        compiler_params=params(60),
    )(tokens, shift[None], scale[None])


def modulate_far_kernel(tokens_ref, pair_ref, out_ref):
    out_ref[...] = normalize(tokens_ref[...], pair_ref[0], pair_ref[1])


def modulate_far(tokens, pair):
    return pl.pallas_call(
        modulate_far_kernel,
        out_shape=jax.ShapeDtypeStruct(tokens.shape, BF16),
        compiler_params=params(8),
    )(tokens, pair)


STEPS = 4


def project_kernel(tokens_refs, weight_ref, q_gain_ref, k_gain_ref, q_ref, kv_ref, *scratch):
    total, weights, gains, weight_sem, gain_sem = scratch
    step = pl.program_id(0)
    depth = tokens_refs[0].shape[1]

    def weight_copy(i):
        rows = pl.ds(pl.multiple_of(i * depth, depth), depth)
        return pltpu.make_async_copy(weight_ref.at[:, rows], weights.at[i], weight_sem.at[i])

    gain_copies = [
        pltpu.make_async_copy(source, gains.at[i], gain_sem.at[i])
        for i, source in enumerate((q_gain_ref, k_gain_ref))
    ]

    @pl.when(step == 0)
    def _():
        for i in range(STEPS):
            weight_copy(i).start()
        for copy in gain_copies:
            copy.start()
        total[...] = jnp.zeros_like(total)

    weight_copy(step).wait()
    tokens = jnp.concatenate([ref[...] for ref in tokens_refs], axis=0)
    weight = jnp.concatenate([weights[step, i] for i in range(3)], axis=1)
    total[...] += jnp.dot(tokens, weight, preferred_element_type=F32)

    @pl.when(step == STEPS - 1)
    def _():
        for copy in gain_copies:
            copy.wait()

        def normed(i, gain):
            part = total[:, i * HD : (i + 1) * HD]
            meansq = jnp.mean(part * part, axis=-1, keepdims=True)
            return part * lax.rsqrt(meansq + epsilon) * gain

        queries = normed(0, gains[0] * (math.log2(math.e) / math.sqrt(HD))).astype(BF16)
        for i in range(q_ref.shape[0]):
            q_ref[i] = queries
        kv_ref[:, :HD] = normed(1, gains[1]).astype(BF16)
        kv_ref[:, HD:] = total[:, 2 * HD :].astype(BF16)


def project(tokens, weight, q_gain, k_gain, copies):
    width = tokens[0].shape[1]
    rows = sum(part.shape[0] for part in tokens)
    depth = width // STEPS
    count = len(tokens)
    return pl.pallas_call(
        lambda *refs: project_kernel(refs[:count], *refs[count:]),
        grid=(STEPS,),
        in_specs=[pl.BlockSpec((part.shape[0], depth), lambda i: (0, i)) for part in tokens]
        + [pl.BlockSpec(memory_space=pltpu.HBM)] * 3,
        out_specs=[
            pl.BlockSpec((copies, rows, HD), lambda i: (0, 0, 0)),
            pl.BlockSpec((rows, 2 * HD), lambda i: (0, 0)),
        ],
        out_shape=[
            jax.ShapeDtypeStruct((copies, rows, HD), BF16),
            jax.ShapeDtypeStruct((rows, 2 * HD), BF16),
        ],
        scratch_shapes=[
            pltpu.VMEM((rows, 3 * HD), F32),
            pltpu.VMEM((STEPS, 3, depth, HD), BF16),
            pltpu.VMEM((2, 1, HD), F32),
            pltpu.SemaphoreType.DMA((STEPS,)),
            pltpu.SemaphoreType.DMA((2,)),
        ],
        compiler_params=params(16),
        cost_estimate=pl.CostEstimate(
            flops=2 * rows * width * 3 * HD, bytes_accessed=3 * width * HD * 2, transcendentals=0
        ),
    )(*tokens, weight, q_gain[None], k_gain[None])


TAIL = 16


def diagonal(rows):
    down = lax.broadcasted_iota(jnp.int32, (rows, HD), 0)
    return down == lax.broadcasted_iota(jnp.int32, (rows, HD), 1)


def row_blocks(rows):
    return [(at, min(HD, rows - at)) for at in range(0, rows, HD)]


def tail_of(rows):
    row_of = lax.broadcasted_iota(jnp.int32, (TAIL, HD), 0)
    tail = jnp.zeros((TAIL, HD), F32)
    for j, row in enumerate(rows):
        high = row.astype(BF16).astype(F32)
        tail = jnp.where(row_of == j, high, tail)
        tail = jnp.where(row_of == len(rows) + j, row - high, tail)
    return tail.astype(BF16)


def totals_of(block, rows):
    count = len(row_blocks(rows))
    starts = [rows + j for j in range(count)]
    return [block[at : at + 1] + block[at + count : at + count + 1] for at in starts]


def attend_kernel(q_ref, kv_ref, out_ref):
    blocks, rows, _ = q_ref.shape
    step = kv_ref.shape[0] // 2
    totals = [0.0] * blocks
    for at in range(0, kv_ref.shape[0], step):
        values = jnp.concatenate([kv_ref[at : at + step, HD:], jnp.ones((step, HD), BF16)], axis=1)
        for i in range(blocks):
            scores = lax.dot_general(
                q_ref[i],
                kv_ref[at : at + step, :HD],
                (((1,), (1,)), ((), ())),
                preferred_element_type=F32,
            )
            weights = jnp.exp2(scores).astype(BF16)
            totals[i] += jnp.dot(weights, values, preferred_element_type=F32)
    for i, total in enumerate(totals):
        out_ref[i, :rows] = total[:, :HD].astype(BF16)
        sums = [
            jnp.where(diagonal(size), total[at : at + size, HD:], 0.0)
            for at, size in row_blocks(rows)
        ]
        out_ref[i, rows:] = tail_of([jnp.sum(square, axis=0, keepdims=True) for square in sums])


def attend(queries, keyval):
    blocks, rows, _ = queries.shape
    keys = keyval.shape[0]
    return pl.pallas_call(
        attend_kernel,
        grid=(blocks // 2,),
        in_specs=[
            pl.BlockSpec((2, rows, HD), lambda i: (i, 0, 0)),
            pl.BlockSpec(keyval.shape, lambda i: (0, 0)),
        ],
        out_specs=pl.BlockSpec((2, rows + TAIL, HD), lambda i: (i, 0, 0)),
        out_shape=jax.ShapeDtypeStruct((blocks, rows + TAIL, HD), BF16),
        compiler_params=params(16),
        cost_estimate=pl.CostEstimate(
            flops=5 * blocks * rows * keys * HD,
            bytes_accessed=4 * keys * HD,
            transcendentals=blocks * rows * keys,
        ),
    )(queries, keyval)


def divide_kernel(partial_ref, out_ref):
    rows = partial_ref.shape[1] - TAIL
    summed = jnp.sum(partial_ref[...].astype(F32), axis=0)
    attended = []
    for row, (at, size) in zip(totals_of(summed, rows), row_blocks(rows)):
        square = jnp.broadcast_to(row, (size, HD))
        column = jnp.sum(jnp.where(diagonal(size), square, 0.0), axis=1, keepdims=True)
        attended.append((summed[at : at + size] / column).astype(BF16))
    attended = jnp.concatenate(attended, axis=0)
    along, part = out_ref.shape[0], out_ref.shape[1] // 4
    for y in range(along):
        for far in range(2):
            for other in range(2):
                at = ((far * 2 + other) * along + y) * part
                to = (other * 2 + far) * part
                out_ref[y, to : to + part] = attended[at : at + part]


def divide(partial, along):
    rows = partial.shape[1] - TAIL
    return pl.pallas_call(
        divide_kernel,
        out_shape=jax.ShapeDtypeStruct((along, rows // along, HD), BF16),
        compiler_params=params(8),
    )(partial)


def mix_kernel(y_ref, attended_ref, first_ref, *refs):
    *weight_refs, own_ref, other_ref, first, first_sem = refs
    copy = pltpu.make_async_copy(first_ref, first, first_sem.at[0])
    copy.start()
    mixed = jnp.dot(
        jnp.concatenate([attended_ref[y_ref[0] ^ i] for i in (2, 3)], axis=1),
        jnp.concatenate([ref[...] for ref in weight_refs[1:]], axis=0),
        preferred_element_type=F32,
    )
    copy.wait()
    mixed += jnp.dot(
        jnp.concatenate([attended_ref[y_ref[0] ^ i] for i in (0, 1)], axis=1),
        jnp.concatenate([first[...], weight_refs[0][...]], axis=0),
        preferred_element_type=F32,
    )
    half = own_ref.shape[0]
    own_ref[...] = mixed[:half]
    other_ref[...] = mixed[half:].astype(BF16)


def mix(y, attended, weights):
    rows = attended.shape[1]
    depth, width = weights[0].shape
    vmem = pl.BlockSpec(memory_space=pltpu.VMEM)
    return pl.pallas_call(
        mix_kernel,
        in_specs=[
            pl.BlockSpec(memory_space=pltpu.SMEM),
            vmem,
            pl.BlockSpec(memory_space=pltpu.HBM),
            vmem,
            vmem,
            vmem,
        ],
        out_shape=[
            jax.ShapeDtypeStruct((rows // 2, width), F32),
            jax.ShapeDtypeStruct((rows // 2, width), BF16),
        ],
        scratch_shapes=[pltpu.VMEM((depth, width), BF16), pltpu.SemaphoreType.DMA((1,))],
        compiler_params=params(16),
        cost_estimate=pl.CostEstimate(
            flops=2 * len(weights) * rows * width * depth,
            bytes_accessed=2 * len(weights) * width * depth,
            transcendentals=0,
        ),
    )(y, attended, *weights)


def local(tokens, mod_shift, mod_scale, qkv_weight, q_gain, k_gain, out_weight, out_gate):
    rows, width = tokens.shape

    def along_y(block, distance):
        return lax.ppermute(block, "y", [(i, i ^ distance) for i in range(4)])

    def spread(modulated):
        own = lax.all_gather(modulated, "y", axis=0, tiled=True)
        return [own, swap(own, "core")]

    far = trade_halves(tokens)
    near, pair = modulate_near(tokens, mod_shift, mod_scale)
    parts = spread(near) + spread(modulate_far(far, pair))
    queries, keyval = project(parts, qkv_weight, q_gain, k_gain, 8)
    out_weight, keyval = lax.optimization_barrier((out_weight, keyval))
    weights = [out_weight] + [along_y(out_weight, i) for i in (1, 2, 3)]
    queries = lax.all_to_all(queries, NEAR, 0, 0)
    one, two = swap(keyval, "za"), swap(keyval, "zb")
    three = swap(one, "zb")
    partial = attend(queries, jnp.concatenate([keyval, one, two, three], axis=0))
    partial, weights = lax.optimization_barrier((partial, weights))
    partial = lax.all_to_all(partial, NEAR, 0, 0)
    attended = lax.all_to_all(divide(partial, 4), "y", 0, 0)
    y = lax.axis_index("y").astype(jnp.int32).reshape(1)
    own, other = mix(y, attended, weights)
    summed = own + swap(other, "core").astype(F32)
    arrived = trade_halves(summed[rows:].astype(BF16)).astype(F32)
    return ((summed[:rows] + arrived) * out_gate).astype(BF16)


def solution(mesh):
    fine = Mesh(mesh.devices.reshape(tuple(AXES.values())), ALL)
    heads = ("y", "zh", "core")
    return jax.shard_map(
        local,
        mesh=fine,
        in_specs=(
            P(ALL, None),
            P(),
            P(),
            P(None, None, heads),
            P(),
            P(),
            P(heads, None),
            P(),
        ),
        out_specs=P(ALL, None),
        check_vma=False,
    )
```

```python
import math

import jax
import jax.numpy as jnp
from jax import lax
from jax.experimental import pallas as pl
from jax.experimental.pallas import tpu as pltpu
from jax.sharding import Mesh, PartitionSpec as P

HD = 128
epsilon = 1e-06
AXES = {"y": 4, "zh": 2, "core": 2, "za": 2, "zb": 2, "zc": 2, "x": 4}
ALL = tuple(AXES)
NEAR = ("zc", "x")
F32 = jnp.float32
BF16 = jnp.bfloat16
MIB = 1 << 20


def params(mib):
    return pltpu.CompilerParams(vmem_limit_bytes=mib * MIB)


def swap(block, axis):
    return lax.ppermute(block, axis, [(0, 1), (1, 0)])


def trade_halves(block):
    return lax.ppermute(block, ("zh", "za"), [(i, i ^ 3) for i in range(4)])


def normalize(tokens, shift, scale):
    widened = tokens.astype(F32)
    center = widened - jnp.mean(widened, axis=-1, keepdims=True)
    spread = jnp.mean(center * center, axis=-1, keepdims=True)
    normed = center * lax.rsqrt(spread + epsilon)
    return (normed * scale + shift).astype(BF16)


def modulate_near_kernel(tokens_ref, *refs):
    *row_refs, out_ref, rows_ref, tokens, sem = refs
    copies = [pltpu.make_async_copy(tokens_ref, tokens, sem.at[0])]
    for i, ref in enumerate(row_refs):
        copies.append(
            pltpu.make_async_copy(ref, rows_ref.at[i, :, pl.ds(0, ref.shape[1])], sem.at[i + 1])
        )
    for copy in copies:
        copy.start()
    for copy in copies:
        copy.wait()
    out_ref[...] = normalize(tokens[...], rows_ref[0], rows_ref[1])


def modulate_near(tokens, rows):
    width = tokens.shape[1]
    return pl.pallas_call(
        modulate_near_kernel,
        in_specs=[pl.BlockSpec(memory_space=pltpu.HBM)] * (1 + len(rows)),
        out_specs=[pl.BlockSpec(memory_space=pltpu.VMEM)] * 2,
        out_shape=[
            jax.ShapeDtypeStruct(tokens.shape, BF16),
            jax.ShapeDtypeStruct((len(rows), 1, width), F32),
        ],
        scratch_shapes=[
            pltpu.VMEM(tokens.shape, BF16),
            pltpu.SemaphoreType.DMA((1 + len(rows),)),
        ],
        compiler_params=params(60),
    )(tokens, *[row[None] for row in rows])


def modulate_far_kernel(tokens_ref, rows_ref, out_ref, gains_ref):
    out_ref[...] = normalize(tokens_ref[...], rows_ref[0], rows_ref[1])
    gains_ref[...] = rows_ref[2:, :, :HD]


def modulate_far(tokens, rows):
    return pl.pallas_call(
        modulate_far_kernel,
        out_shape=[
            jax.ShapeDtypeStruct(tokens.shape, BF16),
            jax.ShapeDtypeStruct((2, 1, HD), F32),
        ],
        compiler_params=params(8),
    )(tokens, rows)


STEPS = 4


def project_kernel(tokens_refs, gains_ref, weight_ref, q_ref, kv_ref, weights, sem):
    depth = weights.shape[2]
    copies = [
        pltpu.make_async_copy(
            weight_ref.at[:, pl.ds(i * depth, depth)], weights.at[i], sem.at[i]
        )
        for i in range(STEPS)
    ]
    for copy in copies:
        copy.start()
    total = 0.0
    for i, copy in enumerate(copies):
        tokens = [ref[:, i * depth : (i + 1) * depth] for ref in tokens_refs]
        tokens = jnp.concatenate(tokens, axis=0)
        copy.wait()
        weight = jnp.concatenate([weights[i, j] for j in range(3)], axis=1)
        total += jnp.dot(tokens, weight, preferred_element_type=F32)

    def normed(i, gain):
        part = total[:, i * HD : (i + 1) * HD]
        meansq = jnp.mean(part * part, axis=-1, keepdims=True)
        return part * lax.rsqrt(meansq + epsilon) * gain

    kv_ref[:, :HD] = normed(1, gains_ref[1]).astype(BF16)
    kv_ref[:, HD:] = total[:, 2 * HD :].astype(BF16)
    queries = normed(0, gains_ref[0] * (math.log2(math.e) / math.sqrt(HD))).astype(BF16)
    for i in range(q_ref.shape[0]):
        q_ref[i] = queries


def project(tokens, gains, weight, copies):
    width = tokens[0].shape[1]
    rows = sum(part.shape[0] for part in tokens)
    count = len(tokens)
    vmem = pl.BlockSpec(memory_space=pltpu.VMEM)
    return pl.pallas_call(
        lambda *refs: project_kernel(refs[:count], *refs[count:]),
        in_specs=[vmem] * (count + 1) + [pl.BlockSpec(memory_space=pltpu.HBM)],
        out_specs=[vmem, vmem],
        out_shape=[
            jax.ShapeDtypeStruct((copies, rows, HD), BF16),
            jax.ShapeDtypeStruct((rows, 2 * HD), BF16),
        ],
        scratch_shapes=[
            pltpu.VMEM((STEPS, 3, width // STEPS, HD), BF16),
            pltpu.SemaphoreType.DMA((STEPS,)),
        ],
        compiler_params=params(50),
        cost_estimate=pl.CostEstimate(
            flops=2 * rows * width * 3 * HD, bytes_accessed=3 * width * HD * 2, transcendentals=0
        ),
    )(*tokens, gains, weight)


TAIL = 16


def diagonal(rows):
    down = lax.broadcasted_iota(jnp.int32, (rows, HD), 0)
    return down == lax.broadcasted_iota(jnp.int32, (rows, HD), 1)


def row_blocks(rows):
    return [(at, min(HD, rows - at)) for at in range(0, rows, HD)]


def tail_of(rows):
    row_of = lax.broadcasted_iota(jnp.int32, (TAIL, HD), 0)
    tail = jnp.zeros((TAIL, HD), F32)
    for j, row in enumerate(rows):
        high = row.astype(BF16).astype(F32)
        tail = jnp.where(row_of == j, high, tail)
        tail = jnp.where(row_of == len(rows) + j, row - high, tail)
    return tail.astype(BF16)


def totals_of(block, rows):
    count = len(row_blocks(rows))
    starts = [rows + j for j in range(count)]
    return [block[at : at + 1] + block[at + count : at + count + 1] for at in starts]


def attend_kernel(q_ref, kv_ref, out_ref):
    blocks, rows, _ = q_ref.shape
    step = kv_ref.shape[0] // 2

    @pl.loop(0, blocks, step=2)
    def _(first):
        totals = [0.0, 0.0]
        for at in range(0, kv_ref.shape[0], step):
            ones = jnp.ones((step, HD), BF16)
            values = jnp.concatenate([kv_ref[at : at + step, HD:], ones], axis=1)
            for i in range(2):
                scores = lax.dot_general(
                    q_ref[first + i],
                    kv_ref[at : at + step, :HD],
                    (((1,), (1,)), ((), ())),
                    preferred_element_type=F32,
                )
                weights = jnp.exp2(scores).astype(BF16)
                totals[i] += jnp.dot(weights, values, preferred_element_type=F32)
        for i, total in enumerate(totals):
            out_ref[first + i, :rows] = total[:, :HD].astype(BF16)
            sums = [
                jnp.where(diagonal(size), total[at : at + size, HD:], 0.0)
                for at, size in row_blocks(rows)
            ]
            out_ref[first + i, rows:] = tail_of(
                [jnp.sum(square, axis=0, keepdims=True) for square in sums]
            )


def attend(queries, keyval):
    blocks, rows, _ = queries.shape
    keys = keyval.shape[0]
    vmem = pl.BlockSpec(memory_space=pltpu.VMEM)
    return pl.pallas_call(
        attend_kernel,
        in_specs=[vmem, vmem],
        out_specs=vmem,
        out_shape=jax.ShapeDtypeStruct((blocks, rows + TAIL, HD), BF16),
        compiler_params=params(16),
        cost_estimate=pl.CostEstimate(
            flops=4 * blocks * rows * keys * HD,
            bytes_accessed=4 * keys * HD,
            transcendentals=blocks * rows * keys,
        ),
    )(queries, keyval)


def divide_kernel(partial_ref, out_ref):
    rows = partial_ref.shape[1] - TAIL
    summed = jnp.sum(partial_ref[...].astype(F32), axis=0)
    attended = []
    for row, (at, size) in zip(totals_of(summed, rows), row_blocks(rows)):
        square = jnp.broadcast_to(row, (size, HD))
        column = jnp.sum(jnp.where(diagonal(size), square, 0.0), axis=1, keepdims=True)
        attended.append((summed[at : at + size] / column).astype(BF16))
    attended = jnp.concatenate(attended, axis=0)
    along, part = out_ref.shape[0], out_ref.shape[1] // 4
    for y in range(along):
        for far in range(2):
            for other in range(2):
                at = ((other * 2 + far) * along + y) * part
                to = (other * 2 + far) * part
                out_ref[y, to : to + part] = attended[at : at + part]


def divide(partial, along):
    rows = partial.shape[1] - TAIL
    return pl.pallas_call(
        divide_kernel,
        out_shape=jax.ShapeDtypeStruct((along, rows // along, HD), BF16),
        compiler_params=params(8),
    )(partial)


def mix_kernel(y_ref, attended_ref, first_ref, *refs):
    *weight_refs, own_ref, other_ref, first, first_sem = refs
    copy = pltpu.make_async_copy(first_ref, first, first_sem.at[0])
    copy.start()
    attended = jnp.concatenate([attended_ref[y_ref[0] ^ i] for i in range(4)], axis=1)
    half, width = own_ref.shape
    step = width // 4
    copy.wait()
    for at in range(0, width, step):
        weight = [ref[:, at : at + step] for ref in (first, *weight_refs)]
        weight = jnp.concatenate(weight, axis=0)
        mixed = jnp.dot(attended, weight, preferred_element_type=F32)
        own_ref[:, at : at + step] = mixed[:half]
        other_ref[:, at : at + step] = mixed[half:].astype(BF16)


def mix(y, attended, weights):
    rows = attended.shape[1]
    depth, width = weights[0].shape
    vmem = pl.BlockSpec(memory_space=pltpu.VMEM)
    return pl.pallas_call(
        mix_kernel,
        in_specs=[
            pl.BlockSpec(memory_space=pltpu.SMEM),
            vmem,
            pl.BlockSpec(memory_space=pltpu.HBM),
            vmem,
            vmem,
            vmem,
        ],
        out_shape=[
            jax.ShapeDtypeStruct((rows // 2, width), F32),
            jax.ShapeDtypeStruct((rows // 2, width), BF16),
        ],
        scratch_shapes=[pltpu.VMEM((depth, width), BF16), pltpu.SemaphoreType.DMA((1,))],
        compiler_params=params(16),
        cost_estimate=pl.CostEstimate(
            flops=2 * len(weights) * rows * width * depth,
            bytes_accessed=2 * len(weights) * width * depth,
            transcendentals=0,
        ),
    )(y, attended, *weights)


def local(tokens, mod_shift, mod_scale, qkv_weight, q_gain, k_gain, out_weight, out_gate):
    rows, width = tokens.shape

    def along_y(block, distance):
        return lax.ppermute(block, "y", [(i, i ^ distance) for i in range(4)])

    def spread(modulated):
        return lax.all_gather(modulated, "y", axis=0, tiled=True)

    far = trade_halves(tokens)
    near, rows_held = modulate_near(tokens, [mod_shift, mod_scale, q_gain, k_gain])
    far, gains = modulate_far(far, rows_held)
    own = jnp.concatenate([spread(near), spread(far)], axis=0)
    queries, keyval = project([own, swap(own, "core")], gains, qkv_weight, 8)
    out_weight, keyval = lax.optimization_barrier((out_weight, keyval))
    weights = [out_weight] + [along_y(out_weight, i) for i in (1, 2, 3)]
    queries = lax.all_to_all(queries, NEAR, 0, 0)
    one, two = swap(keyval, "za"), swap(keyval, "zb")
    three = swap(one, "zb")
    partial = attend(queries, jnp.concatenate([keyval, one, two, three], axis=0))
    partial, weights[1], weights[3] = lax.optimization_barrier((partial, weights[1], weights[3]))
    partial = lax.all_to_all(partial, NEAR, 0, 0)
    attended = lax.all_to_all(divide(partial, 4), "y", 0, 0)
    y = lax.axis_index("y").astype(jnp.int32).reshape(1)
    own, other = mix(y, attended, weights)
    summed = own + swap(other, "core").astype(F32)
    arrived = trade_halves(summed[rows:].astype(BF16)).astype(F32)
    return ((summed[:rows] + arrived) * out_gate).astype(BF16)


def solution(mesh):
    fine = Mesh(mesh.devices.reshape(tuple(AXES.values())), ALL)
    heads = ("y", "zh", "core")
    return jax.shard_map(
        local,
        mesh=fine,
        in_specs=(
            P(ALL, None),
            P(),
            P(),
            P(None, None, heads),
            P(),
            P(),
            P(heads, None),
            P(),
        ),
        out_specs=P(ALL, None),
        check_vma=False,
    )
```

```python
import math

import jax
import jax.numpy as jnp
from jax import lax
from jax.experimental import pallas as pl
from jax.experimental.pallas import tpu as pltpu
from jax.sharding import Mesh, PartitionSpec as P

HD = 128
epsilon = 1e-06
AXES = {"y": 4, "zh": 2, "core": 2, "za": 2, "zb": 2, "zc": 2, "x": 4}
ALL = tuple(AXES)
NEAR = ("zc", "x")
F32 = jnp.float32
BF16 = jnp.bfloat16
MIB = 1 << 20


def params(mib):
    return pltpu.CompilerParams(vmem_limit_bytes=mib * MIB)


def swap(block, axis):
    return lax.ppermute(block, axis, [(0, 1), (1, 0)])


def trade_halves(block):
    return lax.ppermute(block, ("zh", "za"), [(i, i ^ 3) for i in range(4)])


def normalize(tokens, shift, scale):
    widened = tokens.astype(F32)
    center = widened - jnp.mean(widened, axis=-1, keepdims=True)
    spread = jnp.mean(center * center, axis=-1, keepdims=True)
    normed = center * lax.rsqrt(spread + epsilon)
    return (normed * scale + shift).astype(BF16)


def modulate_near_kernel(tokens_ref, *refs):
    *row_refs, out_ref, rows_ref, tokens, sem = refs
    copies = [pltpu.make_async_copy(tokens_ref, tokens, sem.at[0])]
    for i, ref in enumerate(row_refs):
        copies.append(
            pltpu.make_async_copy(ref, rows_ref.at[i, :, pl.ds(0, ref.shape[1])], sem.at[i + 1])
        )
    for copy in copies:
        copy.start()
    for copy in copies:
        copy.wait()
    out_ref[...] = normalize(tokens[...], rows_ref[0], rows_ref[1])


def modulate_near(tokens, rows):
    width = tokens.shape[1]
    return pl.pallas_call(
        modulate_near_kernel,
        in_specs=[pl.BlockSpec(memory_space=pltpu.HBM)] * (1 + len(rows)),
        out_specs=[pl.BlockSpec(memory_space=pltpu.VMEM)] * 2,
        out_shape=[
            jax.ShapeDtypeStruct(tokens.shape, BF16),
            jax.ShapeDtypeStruct((len(rows), 1, width), F32),
        ],
        scratch_shapes=[
            pltpu.VMEM(tokens.shape, BF16),
            pltpu.SemaphoreType.DMA((1 + len(rows),)),
        ],
        compiler_params=params(60),
    )(tokens, *[row[None] for row in rows])


def modulate_far_kernel(tokens_ref, rows_ref, out_ref, gains_ref):
    out_ref[...] = normalize(tokens_ref[...], rows_ref[0], rows_ref[1])
    gains_ref[...] = rows_ref[2:, :, :HD]


def modulate_far(tokens, rows):
    return pl.pallas_call(
        modulate_far_kernel,
        out_shape=[
            jax.ShapeDtypeStruct(tokens.shape, BF16),
            jax.ShapeDtypeStruct((2, 1, HD), F32),
        ],
        compiler_params=params(8),
    )(tokens, rows)


STEPS = 4


def project_kernel(tokens_refs, gains_ref, weight_ref, q_ref, kv_ref, weights, sem):
    depth = weights.shape[2]
    copies = [
        pltpu.make_async_copy(
            weight_ref.at[:, pl.ds(i * depth, depth)], weights.at[i], sem.at[i]
        )
        for i in range(STEPS)
    ]
    for copy in copies:
        copy.start()
    total = 0.0
    for i, copy in enumerate(copies):
        tokens = [ref[:, i * depth : (i + 1) * depth] for ref in tokens_refs]
        tokens = jnp.concatenate(tokens, axis=0)
        copy.wait()
        weight = jnp.concatenate([weights[i, j] for j in range(3)], axis=1)
        total += jnp.dot(tokens, weight, preferred_element_type=F32)

    def normed(i, gain):
        part = total[:, i * HD : (i + 1) * HD]
        meansq = jnp.mean(part * part, axis=-1, keepdims=True)
        return part * lax.rsqrt(meansq + epsilon) * gain

    kv_ref[:, :HD] = normed(1, gains_ref[1]).astype(BF16)
    kv_ref[:, HD:] = total[:, 2 * HD :].astype(BF16)
    queries = normed(0, gains_ref[0] * (math.log2(math.e) / math.sqrt(HD))).astype(BF16)
    for i in range(q_ref.shape[0]):
        q_ref[i] = queries


def project(tokens, gains, weight, copies):
    width = tokens[0].shape[1]
    rows = sum(part.shape[0] for part in tokens)
    count = len(tokens)
    vmem = pl.BlockSpec(memory_space=pltpu.VMEM)
    return pl.pallas_call(
        lambda *refs: project_kernel(refs[:count], *refs[count:]),
        in_specs=[vmem] * (count + 1) + [pl.BlockSpec(memory_space=pltpu.HBM)],
        out_specs=[vmem, vmem],
        out_shape=[
            jax.ShapeDtypeStruct((copies, rows, HD), BF16),
            jax.ShapeDtypeStruct((rows, 2 * HD), BF16),
        ],
        scratch_shapes=[
            pltpu.VMEM((STEPS, 3, width // STEPS, HD), BF16),
            pltpu.SemaphoreType.DMA((STEPS,)),
        ],
        compiler_params=params(50),
        cost_estimate=pl.CostEstimate(
            flops=2 * rows * width * 3 * HD, bytes_accessed=3 * width * HD * 2, transcendentals=0
        ),
    )(*tokens, gains, weight)


TAIL = 16


def diagonal(rows):
    down = lax.broadcasted_iota(jnp.int32, (rows, HD), 0)
    return down == lax.broadcasted_iota(jnp.int32, (rows, HD), 1)


def row_blocks(rows):
    return [(at, min(HD, rows - at)) for at in range(0, rows, HD)]


def tail_of(rows):
    row_of = lax.broadcasted_iota(jnp.int32, (TAIL, HD), 0)
    tail = jnp.zeros((TAIL, HD), F32)
    for j, row in enumerate(rows):
        high = row.astype(BF16).astype(F32)
        tail = jnp.where(row_of == j, high, tail)
        tail = jnp.where(row_of == len(rows) + j, row - high, tail)
    return tail.astype(BF16)


def totals_of(block, rows):
    count = len(row_blocks(rows))
    starts = [rows + j for j in range(count)]
    return [block[at : at + 1] + block[at + count : at + count + 1] for at in starts]


def attend_kernel(q_ref, kv_ref, out_ref):
    blocks, rows, _ = q_ref.shape
    step = kv_ref.shape[0] // 2

    @pl.loop(0, blocks, step=2)
    def _(first):
        totals = [0.0, 0.0]
        for at in range(0, kv_ref.shape[0], step):
            ones = jnp.ones((step, HD), BF16)
            values = jnp.concatenate([kv_ref[at : at + step, HD:], ones], axis=1)
            for i in range(2):
                scores = lax.dot_general(
                    q_ref[first + i],
                    kv_ref[at : at + step, :HD],
                    (((1,), (1,)), ((), ())),
                    preferred_element_type=F32,
                )
                weights = jnp.exp2(scores).astype(BF16)
                totals[i] += jnp.dot(weights, values, preferred_element_type=F32)
        for i, total in enumerate(totals):
            out_ref[first + i, :rows] = total[:, :HD].astype(BF16)
            sums = [
                jnp.where(diagonal(size), total[at : at + size, HD:], 0.0)
                for at, size in row_blocks(rows)
            ]
            out_ref[first + i, rows:] = tail_of(
                [jnp.sum(square, axis=0, keepdims=True) for square in sums]
            )


def attend(queries, keyval):
    blocks, rows, _ = queries.shape
    keys = keyval.shape[0]
    vmem = pl.BlockSpec(memory_space=pltpu.VMEM)
    return pl.pallas_call(
        attend_kernel,
        in_specs=[vmem, vmem],
        out_specs=vmem,
        out_shape=jax.ShapeDtypeStruct((blocks, rows + TAIL, HD), BF16),
        compiler_params=params(16),
        cost_estimate=pl.CostEstimate(
            flops=4 * blocks * rows * keys * HD,
            bytes_accessed=4 * keys * HD,
            transcendentals=blocks * rows * keys,
        ),
    )(queries, keyval)


def divide_kernel(partial_ref, out_ref):
    rows = partial_ref.shape[1] - TAIL
    summed = jnp.sum(partial_ref[...].astype(F32), axis=0)
    attended = []
    for row, (at, size) in zip(totals_of(summed, rows), row_blocks(rows)):
        square = jnp.broadcast_to(row, (size, HD))
        column = jnp.sum(jnp.where(diagonal(size), square, 0.0), axis=1, keepdims=True)
        attended.append((summed[at : at + size] / column).astype(BF16))
    attended = jnp.concatenate(attended, axis=0)
    along, part = out_ref.shape[0], out_ref.shape[1] // 4
    for y in range(along):
        for far in range(2):
            for other in range(2):
                at = ((other * 2 + far) * along + y) * part
                to = (other * 2 + far) * part
                out_ref[y, to : to + part] = attended[at : at + part]


def divide(partial, along):
    rows = partial.shape[1] - TAIL
    return pl.pallas_call(
        divide_kernel,
        out_shape=jax.ShapeDtypeStruct((along, rows // along, HD), BF16),
        compiler_params=params(8),
    )(partial)


def mix_kernel(y_ref, attended_ref, first_ref, *refs):
    *weight_refs, own_ref, other_ref, first, first_sem = refs
    copy = pltpu.make_async_copy(first_ref, first, first_sem.at[0])
    copy.start()
    attended = jnp.concatenate([attended_ref[y_ref[0] ^ i] for i in (0, 1, 3, 2)], axis=1)
    half, width = own_ref.shape
    step = width // 4
    copy.wait()
    for at in range(0, width, step):
        weight = [ref[:, at : at + step] for ref in (first, *weight_refs)]
        weight = jnp.concatenate(weight, axis=0)
        mixed = jnp.dot(attended, weight, preferred_element_type=F32)
        own_ref[:, at : at + step] = mixed[:half]
        other_ref[:, at : at + step] = mixed[half:].astype(BF16)


def mix(y, attended, weights):
    rows = attended.shape[1]
    depth, width = weights[0].shape
    vmem = pl.BlockSpec(memory_space=pltpu.VMEM)
    return pl.pallas_call(
        mix_kernel,
        in_specs=[
            pl.BlockSpec(memory_space=pltpu.SMEM),
            vmem,
            pl.BlockSpec(memory_space=pltpu.HBM),
        ]
        + [vmem] * (len(weights) - 1),
        out_shape=[
            jax.ShapeDtypeStruct((rows // 2, width), F32),
            jax.ShapeDtypeStruct((rows // 2, width), BF16),
        ],
        scratch_shapes=[pltpu.VMEM((depth, width), BF16), pltpu.SemaphoreType.DMA((1,))],
        compiler_params=params(16),
        cost_estimate=pl.CostEstimate(
            flops=8 * rows * width * depth,
            bytes_accessed=8 * width * depth,
            transcendentals=0,
        ),
    )(y, attended, *weights)


def local(tokens, mod_shift, mod_scale, qkv_weight, q_gain, k_gain, out_weight, out_gate):
    rows, width = tokens.shape

    def along_y(block, distance):
        return lax.ppermute(block, "y", [(i, i ^ distance) for i in range(4)])

    def spread(modulated):
        return lax.all_gather(modulated, "y", axis=0, tiled=True)

    far = trade_halves(tokens)
    near, rows_held = modulate_near(tokens, [mod_shift, mod_scale, q_gain, k_gain])
    far, gains = modulate_far(far, rows_held)
    own = jnp.concatenate([spread(near), spread(far)], axis=0)
    queries, keyval = project([own, swap(own, "core")], gains, qkv_weight, 8)
    out_weight, keyval = lax.optimization_barrier((out_weight, keyval))
    half = out_weight.shape[0] // 2
    weights = [along_y(out_weight, i) for i in (1, 3)]
    weights += [along_y(out_weight[:half], 2), along_y(out_weight[half:], 2)]
    queries = lax.all_to_all(queries, NEAR, 0, 0)
    one, two = swap(keyval, "za"), swap(keyval, "zb")
    three = swap(one, "zb")
    partial = attend(queries, jnp.concatenate([keyval, one, two, three], axis=0))
    partial, *weights[:3] = lax.optimization_barrier((partial, *weights[:3]))
    partial = lax.all_to_all(partial, NEAR, 0, 0)
    attended = lax.all_to_all(divide(partial, 4), "y", 0, 0)
    y = lax.axis_index("y").astype(jnp.int32).reshape(1)
    own, other = mix(y, attended, [out_weight, *weights])
    summed = own + swap(other, "core").astype(F32)
    arrived = trade_halves(summed[rows:].astype(BF16)).astype(F32)
    return ((summed[:rows] + arrived) * out_gate).astype(BF16)


def solution(mesh):
    fine = Mesh(mesh.devices.reshape(tuple(AXES.values())), ALL)
    heads = ("y", "zh", "core")
    return jax.shard_map(
        local,
        mesh=fine,
        in_specs=(
            P(ALL, None),
            P(),
            P(),
            P(None, None, heads),
            P(),
            P(),
            P(heads, None),
            P(),
        ),
        out_specs=P(ALL, None),
        check_vma=False,
    )
```

```python
import math

import jax
import jax.numpy as jnp
from jax import lax
from jax.experimental import pallas as pl
from jax.experimental.pallas import tpu as pltpu
from jax.sharding import Mesh, PartitionSpec as P

HD = 128
epsilon = 1e-06
AXES = {"y": 4, "zh": 2, "core": 2, "za": 2, "zb": 2, "zc": 2, "x": 4}
ALL = tuple(AXES)
NEAR = ("zc", "x")
F32 = jnp.float32
BF16 = jnp.bfloat16
MIB = 1 << 20


def params(mib):
    return pltpu.CompilerParams(vmem_limit_bytes=mib * MIB)


def swap(block, axis):
    return lax.ppermute(block, axis, [(0, 1), (1, 0)])


def trade_halves(block):
    return lax.ppermute(block, ("zh", "za"), [(i, i ^ 3) for i in range(4)])


def normalize(tokens, shift, scale):
    widened = tokens.astype(F32)
    center = widened - jnp.mean(widened, axis=-1, keepdims=True)
    spread = jnp.mean(center * center, axis=-1, keepdims=True)
    normed = center * lax.rsqrt(spread + epsilon)
    return (normed * scale + shift).astype(BF16)


def modulate_near_kernel(tokens_ref, *refs):
    *row_refs, out_ref, rows_ref, tokens, sem = refs
    copies = [pltpu.make_async_copy(tokens_ref, tokens, sem.at[0])]
    for i, ref in enumerate(row_refs):
        copies.append(
            pltpu.make_async_copy(ref, rows_ref.at[i, :, pl.ds(0, ref.shape[1])], sem.at[i + 1])
        )
    for copy in copies:
        copy.start()
    for copy in copies:
        copy.wait()
    out_ref[...] = normalize(tokens[...], rows_ref[0], rows_ref[1])


def modulate_near(tokens, rows):
    width = tokens.shape[1]
    return pl.pallas_call(
        modulate_near_kernel,
        in_specs=[pl.BlockSpec(memory_space=pltpu.HBM)] * (1 + len(rows)),
        out_specs=[pl.BlockSpec(memory_space=pltpu.VMEM)] * 2,
        out_shape=[
            jax.ShapeDtypeStruct(tokens.shape, BF16),
            jax.ShapeDtypeStruct((len(rows), 1, width), F32),
        ],
        scratch_shapes=[
            pltpu.VMEM(tokens.shape, BF16),
            pltpu.SemaphoreType.DMA((1 + len(rows),)),
        ],
        compiler_params=params(60),
    )(tokens, *[row[None] for row in rows])


def modulate_far_kernel(tokens_ref, rows_ref, out_ref, gains_ref):
    out_ref[...] = normalize(tokens_ref[...], rows_ref[0], rows_ref[1])
    gains_ref[...] = rows_ref[2:, :, :HD]


def modulate_far(tokens, rows):
    return pl.pallas_call(
        modulate_far_kernel,
        out_shape=[
            jax.ShapeDtypeStruct(tokens.shape, BF16),
            jax.ShapeDtypeStruct((2, 1, HD), F32),
        ],
        compiler_params=params(8),
    )(tokens, rows)


STEPS = 4


def project_kernel(tokens_refs, gains_ref, weight_ref, q_ref, kv_ref, weights, sem):
    depth = weights.shape[2]
    copies = [
        pltpu.make_async_copy(
            weight_ref.at[:, pl.ds(i * depth, depth)], weights.at[i], sem.at[i]
        )
        for i in range(STEPS)
    ]
    for copy in copies:
        copy.start()
    total = 0.0
    for i, copy in enumerate(copies):
        tokens = [ref[:, i * depth : (i + 1) * depth] for ref in tokens_refs]
        tokens = jnp.concatenate(tokens, axis=0)
        copy.wait()
        weight = jnp.concatenate([weights[i, j] for j in range(3)], axis=1)
        total += jnp.dot(tokens, weight, preferred_element_type=F32)

    def normed(i, gain):
        part = total[:, i * HD : (i + 1) * HD]
        meansq = jnp.mean(part * part, axis=-1, keepdims=True)
        return part * lax.rsqrt(meansq + epsilon) * gain

    kv_ref[:, :HD] = normed(1, gains_ref[1]).astype(BF16)
    kv_ref[:, HD:] = total[:, 2 * HD :].astype(BF16)
    queries = normed(0, gains_ref[0] * (math.log2(math.e) / math.sqrt(HD))).astype(BF16)
    for i in range(q_ref.shape[0]):
        q_ref[i] = queries


def project(tokens, gains, weight, copies):
    width = tokens[0].shape[1]
    rows = sum(part.shape[0] for part in tokens)
    count = len(tokens)
    vmem = pl.BlockSpec(memory_space=pltpu.VMEM)
    return pl.pallas_call(
        lambda *refs: project_kernel(refs[:count], *refs[count:]),
        in_specs=[vmem] * (count + 1) + [pl.BlockSpec(memory_space=pltpu.HBM)],
        out_specs=[vmem, vmem],
        out_shape=[
            jax.ShapeDtypeStruct((copies, rows, HD), BF16),
            jax.ShapeDtypeStruct((rows, 2 * HD), BF16),
        ],
        scratch_shapes=[
            pltpu.VMEM((STEPS, 3, width // STEPS, HD), BF16),
            pltpu.SemaphoreType.DMA((STEPS,)),
        ],
        compiler_params=params(50),
        cost_estimate=pl.CostEstimate(
            flops=2 * rows * width * 3 * HD, bytes_accessed=3 * width * HD * 2, transcendentals=0
        ),
    )(*tokens, gains, weight)


TAIL = 16


def diagonal(rows):
    down = lax.broadcasted_iota(jnp.int32, (rows, HD), 0)
    return down == lax.broadcasted_iota(jnp.int32, (rows, HD), 1)


def row_blocks(rows):
    return [(at, min(HD, rows - at)) for at in range(0, rows, HD)]


def tail_of(rows):
    row_of = lax.broadcasted_iota(jnp.int32, (TAIL, HD), 0)
    tail = jnp.zeros((TAIL, HD), F32)
    for j, row in enumerate(rows):
        high = row.astype(BF16).astype(F32)
        tail = jnp.where(row_of == j, high, tail)
        tail = jnp.where(row_of == len(rows) + j, row - high, tail)
    return tail.astype(BF16)


def totals_of(block, rows):
    count = len(row_blocks(rows))
    starts = [rows + j for j in range(count)]
    return [block[at : at + 1] + block[at + count : at + count + 1] for at in starts]


def attend_kernel(q_ref, kv_ref, out_ref):
    blocks, rows, _ = q_ref.shape
    step = kv_ref.shape[0] // 2
    totals = [0.0] * blocks
    for at in range(0, kv_ref.shape[0], step):
        values = jnp.concatenate([kv_ref[at : at + step, HD:], jnp.ones((step, HD), BF16)], axis=1)
        for i in range(blocks):
            scores = lax.dot_general(
                q_ref[i],
                kv_ref[at : at + step, :HD],
                (((1,), (1,)), ((), ())),
                preferred_element_type=F32,
            )
            weights = jnp.exp2(scores).astype(BF16)
            totals[i] += jnp.dot(weights, values, preferred_element_type=F32)
    for i, total in enumerate(totals):
        out_ref[i, :rows] = total[:, :HD].astype(BF16)
        sums = [
            jnp.where(diagonal(size), total[at : at + size, HD:], 0.0)
            for at, size in row_blocks(rows)
        ]
        out_ref[i, rows:] = tail_of([jnp.sum(square, axis=0, keepdims=True) for square in sums])


def attend(queries, keyval):
    blocks, rows, _ = queries.shape
    keys = keyval.shape[0]
    return pl.pallas_call(
        attend_kernel,
        grid=(blocks // 2,),
        in_specs=[
            pl.BlockSpec((2, rows, HD), lambda i: (i, 0, 0)),
            pl.BlockSpec(keyval.shape, lambda i: (0, 0)),
        ],
        out_specs=pl.BlockSpec((2, rows + TAIL, HD), lambda i: (i, 0, 0)),
        out_shape=jax.ShapeDtypeStruct((blocks, rows + TAIL, HD), BF16),
        compiler_params=params(16),
        cost_estimate=pl.CostEstimate(
            flops=4 * blocks * rows * keys * HD,
            bytes_accessed=4 * keys * HD,
            transcendentals=blocks * rows * keys,
        ),
    )(queries, keyval)


def divide_kernel(partial_ref, out_ref):
    rows = partial_ref.shape[1] - TAIL
    summed = jnp.sum(partial_ref[...].astype(F32), axis=0)
    attended = []
    for row, (at, size) in zip(totals_of(summed, rows), row_blocks(rows)):
        square = jnp.broadcast_to(row, (size, HD))
        column = jnp.sum(jnp.where(diagonal(size), square, 0.0), axis=1, keepdims=True)
        attended.append((summed[at : at + size] / column).astype(BF16))
    attended = jnp.concatenate(attended, axis=0)
    along, part = out_ref.shape[0], out_ref.shape[1] // 4
    for y in range(along):
        for far in range(2):
            for other in range(2):
                at = ((other * 2 + far) * along + y) * part
                to = (other * 2 + far) * part
                out_ref[y, to : to + part] = attended[at : at + part]


def divide(partial, along):
    rows = partial.shape[1] - TAIL
    return pl.pallas_call(
        divide_kernel,
        out_shape=jax.ShapeDtypeStruct((along, rows // along, HD), BF16),
        compiler_params=params(8),
    )(partial)


def mix_kernel(y_ref, attended_ref, first_ref, *refs):
    *weight_refs, near_ref, far_ref, near_out_ref, far_out_ref, first, first_sem = refs
    copy = pltpu.make_async_copy(first_ref, first, first_sem.at[0])
    copy.start()
    attended = jnp.concatenate([attended_ref[y_ref[0] ^ i] for i in (0, 1, 3, 2)], axis=1)
    part, width = near_ref.shape
    step = width // 4
    copy.wait()
    for at in range(0, width, step):
        weight = [ref[:, at : at + step] for ref in (first, *weight_refs)]
        weight = jnp.concatenate(weight, axis=0)
        mixed = jnp.dot(attended, weight, preferred_element_type=F32)
        near_ref[:, at : at + step] = mixed[:part]
        far_ref[:, at : at + step] = mixed[part : 2 * part]
        near_out_ref[:, at : at + step] = mixed[2 * part : 3 * part].astype(BF16)
        far_out_ref[:, at : at + step] = mixed[3 * part :].astype(BF16)


def mix(y, attended, weights):
    rows = attended.shape[1]
    depth, width = weights[0].shape
    vmem = pl.BlockSpec(memory_space=pltpu.VMEM)
    return pl.pallas_call(
        mix_kernel,
        in_specs=[
            pl.BlockSpec(memory_space=pltpu.SMEM),
            vmem,
            pl.BlockSpec(memory_space=pltpu.HBM),
        ]
        + [vmem] * (len(weights) - 1),
        out_shape=[
            jax.ShapeDtypeStruct((rows // 4, width), kind) for kind in (F32, F32, BF16, BF16)
        ],
        scratch_shapes=[pltpu.VMEM((depth, width), BF16), pltpu.SemaphoreType.DMA((1,))],
        compiler_params=params(16),
        cost_estimate=pl.CostEstimate(
            flops=8 * rows * width * depth,
            bytes_accessed=8 * width * depth,
            transcendentals=0,
        ),
    )(y, attended, *weights)


def local(tokens, mod_shift, mod_scale, qkv_weight, q_gain, k_gain, out_weight, out_gate):
    width = tokens.shape[1]

    def along_y(block, distance):
        return lax.ppermute(block, "y", [(i, i ^ distance) for i in range(4)])

    def spread(modulated):
        return lax.all_gather(modulated, "y", axis=0, tiled=True)

    far = trade_halves(tokens)
    near, rows_held = modulate_near(tokens, [mod_shift, mod_scale, q_gain, k_gain])
    far, gains = modulate_far(far, rows_held)
    own = jnp.concatenate([spread(near), spread(far)], axis=0)
    queries, keyval = project([own, swap(own, "core")], gains, qkv_weight, 8)
    out_weight, keyval = lax.optimization_barrier((out_weight, keyval))
    half = out_weight.shape[0] // 2
    weights = [along_y(out_weight, i) for i in (1, 3)]
    weights += [along_y(out_weight[:half], 2), along_y(out_weight[half:], 2)]
    queries = lax.all_to_all(queries, NEAR, 0, 0)
    one, two = swap(keyval, "za"), swap(keyval, "zb")
    three = swap(one, "zb")
    partial = attend(queries, jnp.concatenate([keyval, one, two, three], axis=0))
    partial, *weights[:3] = lax.optimization_barrier((partial, *weights[:3]))
    partial = lax.all_to_all(partial, NEAR, 0, 0)
    attended = lax.all_to_all(divide(partial, 4), "y", 0, 0)
    y = lax.axis_index("y").astype(jnp.int32).reshape(1)
    near, far, near_out, far_out = mix(y, attended, [out_weight, *weights])
    far = (far + swap(far_out, "core").astype(F32)).astype(BF16)
    near_out, far = lax.optimization_barrier((near_out, far))
    arrived = trade_halves(far).astype(F32)
    return ((near + swap(near_out, "core").astype(F32) + arrived) * out_gate).astype(BF16)


def solution(mesh):
    fine = Mesh(mesh.devices.reshape(tuple(AXES.values())), ALL)
    heads = ("y", "zh", "core")
    return jax.shard_map(
        local,
        mesh=fine,
        in_specs=(
            P(ALL, None),
            P(),
            P(),
            P(None, None, heads),
            P(),
            P(),
            P(heads, None),
            P(),
        ),
        out_specs=P(ALL, None),
        check_vma=False,
    )
```

```python
import math

import jax
import jax.numpy as jnp
from jax import lax
from jax.experimental import pallas as pl
from jax.experimental.pallas import tpu as pltpu
from jax.sharding import Mesh, PartitionSpec as P

HD = 128
epsilon = 1e-06
AXES = {"y": 4, "zh": 2, "core": 2, "za": 2, "zb": 2, "zc": 2, "x": 4}
ALL = tuple(AXES)
NEAR = ("zc", "x")
F32 = jnp.float32
BF16 = jnp.bfloat16
MIB = 1 << 20


def params(mib):
    return pltpu.CompilerParams(vmem_limit_bytes=mib * MIB)


def swap(block, axis):
    return lax.ppermute(block, axis, [(0, 1), (1, 0)])


def trade_halves(block):
    return lax.ppermute(block, ("zh", "za"), [(i, i ^ 3) for i in range(4)])


def normalize(tokens, shift, scale):
    widened = tokens.astype(F32)
    center = widened - jnp.mean(widened, axis=-1, keepdims=True)
    spread = jnp.mean(center * center, axis=-1, keepdims=True)
    normed = center * lax.rsqrt(spread + epsilon)
    return (normed * scale + shift).astype(BF16)


def modulate_near_kernel(tokens_ref, *refs):
    *row_refs, out_ref, rows_ref, tokens, sem = refs
    copies = [pltpu.make_async_copy(tokens_ref, tokens, sem.at[0])]
    for i, ref in enumerate(row_refs):
        copies.append(
            pltpu.make_async_copy(ref, rows_ref.at[i, :, pl.ds(0, ref.shape[1])], sem.at[i + 1])
        )
    for copy in copies:
        copy.start()
    for copy in copies:
        copy.wait()
    out_ref[...] = normalize(tokens[...], rows_ref[0], rows_ref[1])


def modulate_near(tokens, rows):
    width = tokens.shape[1]
    return pl.pallas_call(
        modulate_near_kernel,
        in_specs=[pl.BlockSpec(memory_space=pltpu.HBM)] * (1 + len(rows)),
        out_specs=[pl.BlockSpec(memory_space=pltpu.VMEM)] * 2,
        out_shape=[
            jax.ShapeDtypeStruct(tokens.shape, BF16),
            jax.ShapeDtypeStruct((len(rows), 1, width), F32),
        ],
        scratch_shapes=[
            pltpu.VMEM(tokens.shape, BF16),
            pltpu.SemaphoreType.DMA((1 + len(rows),)),
        ],
        compiler_params=params(60),
    )(tokens, *[row[None] for row in rows])


def modulate_far_kernel(tokens_ref, rows_ref, out_ref, gains_ref):
    out_ref[...] = normalize(tokens_ref[...], rows_ref[0], rows_ref[1])
    gains_ref[...] = rows_ref[2:, :, :HD]


def modulate_far(tokens, rows):
    return pl.pallas_call(
        modulate_far_kernel,
        out_shape=[
            jax.ShapeDtypeStruct(tokens.shape, BF16),
            jax.ShapeDtypeStruct((2, 1, HD), F32),
        ],
        compiler_params=params(8),
    )(tokens, rows)


STEPS = 4


def project_kernel(tokens_refs, gains_ref, weight_ref, q_ref, kv_ref, weights, sem):
    depth = weights.shape[2]
    copies = [
        pltpu.make_async_copy(
            weight_ref.at[:, pl.ds(i * depth, depth)], weights.at[i], sem.at[i]
        )
        for i in range(STEPS)
    ]
    for copy in copies:
        copy.start()
    total = 0.0
    for i, copy in enumerate(copies):
        tokens = [ref[:, i * depth : (i + 1) * depth] for ref in tokens_refs]
        tokens = jnp.concatenate(tokens, axis=0)
        copy.wait()
        weight = jnp.concatenate([weights[i, j] for j in range(3)], axis=1)
        total += jnp.dot(tokens, weight, preferred_element_type=F32)

    def normed(i, gain):
        part = total[:, i * HD : (i + 1) * HD]
        meansq = jnp.mean(part * part, axis=-1, keepdims=True)
        return part * lax.rsqrt(meansq + epsilon) * gain

    kv_ref[:, :HD] = normed(1, gains_ref[1]).astype(BF16)
    kv_ref[:, HD:] = total[:, 2 * HD :].astype(BF16)
    queries = normed(0, gains_ref[0] * (math.log2(math.e) / math.sqrt(HD))).astype(BF16)
    for i in range(q_ref.shape[0]):
        q_ref[i] = queries


def project(tokens, gains, weight, copies):
    width = tokens[0].shape[1]
    rows = sum(part.shape[0] for part in tokens)
    count = len(tokens)
    vmem = pl.BlockSpec(memory_space=pltpu.VMEM)
    return pl.pallas_call(
        lambda *refs: project_kernel(refs[:count], *refs[count:]),
        in_specs=[vmem] * (count + 1) + [pl.BlockSpec(memory_space=pltpu.HBM)],
        out_specs=[vmem, vmem],
        out_shape=[
            jax.ShapeDtypeStruct((copies, rows, HD), BF16),
            jax.ShapeDtypeStruct((rows, 2 * HD), BF16),
        ],
        scratch_shapes=[
            pltpu.VMEM((STEPS, 3, width // STEPS, HD), BF16),
            pltpu.SemaphoreType.DMA((STEPS,)),
        ],
        compiler_params=params(50),
        cost_estimate=pl.CostEstimate(
            flops=2 * rows * width * 3 * HD, bytes_accessed=3 * width * HD * 2, transcendentals=0
        ),
    )(*tokens, gains, weight)


TAIL = 16


def diagonal(rows):
    down = lax.broadcasted_iota(jnp.int32, (rows, HD), 0)
    return down == lax.broadcasted_iota(jnp.int32, (rows, HD), 1)


def row_blocks(rows):
    return [(at, min(HD, rows - at)) for at in range(0, rows, HD)]


def tail_of(rows):
    row_of = lax.broadcasted_iota(jnp.int32, (TAIL, HD), 0)
    tail = jnp.zeros((TAIL, HD), F32)
    for j, row in enumerate(rows):
        high = row.astype(BF16).astype(F32)
        tail = jnp.where(row_of == j, high, tail)
        tail = jnp.where(row_of == len(rows) + j, row - high, tail)
    return tail.astype(BF16)


def totals_of(block, rows):
    count = len(row_blocks(rows))
    starts = [rows + j for j in range(count)]
    return [block[at : at + 1] + block[at + count : at + count + 1] for at in starts]


def attend_kernel(q_ref, kv_ref, out_ref):
    blocks, rows, _ = q_ref.shape
    step = kv_ref.shape[0] // 2
    totals = [0.0] * blocks
    for at in range(0, kv_ref.shape[0], step):
        values = jnp.concatenate([kv_ref[at : at + step, HD:], jnp.ones((step, HD), BF16)], axis=1)
        for i in range(blocks):
            scores = lax.dot_general(
                q_ref[i],
                kv_ref[at : at + step, :HD],
                (((1,), (1,)), ((), ())),
                preferred_element_type=F32,
            )
            weights = jnp.exp2(scores).astype(BF16)
            totals[i] += jnp.dot(weights, values, preferred_element_type=F32)
    for i, total in enumerate(totals):
        out_ref[i, :rows] = total[:, :HD].astype(BF16)
        sums = [
            jnp.where(diagonal(size), total[at : at + size, HD:], 0.0)
            for at, size in row_blocks(rows)
        ]
        out_ref[i, rows:] = tail_of([jnp.sum(square, axis=0, keepdims=True) for square in sums])


def attend(queries, keyval):
    blocks, rows, _ = queries.shape
    keys = keyval.shape[0]
    return pl.pallas_call(
        attend_kernel,
        grid=(blocks // 2,),
        in_specs=[
            pl.BlockSpec((2, rows, HD), lambda i: (i, 0, 0)),
            pl.BlockSpec(keyval.shape, lambda i: (0, 0)),
        ],
        out_specs=pl.BlockSpec((2, rows + TAIL, HD), lambda i: (i, 0, 0)),
        out_shape=jax.ShapeDtypeStruct((blocks, rows + TAIL, HD), BF16),
        compiler_params=params(16),
        cost_estimate=pl.CostEstimate(
            flops=4 * blocks * rows * keys * HD,
            bytes_accessed=4 * keys * HD,
            transcendentals=blocks * rows * keys,
        ),
    )(queries, keyval)


def divide_kernel(partial_ref, out_ref):
    rows = partial_ref.shape[1] - TAIL
    summed = jnp.sum(partial_ref[...].astype(F32), axis=0)
    attended = []
    for row, (at, size) in zip(totals_of(summed, rows), row_blocks(rows)):
        square = jnp.broadcast_to(row, (size, HD))
        column = jnp.sum(jnp.where(diagonal(size), square, 0.0), axis=1, keepdims=True)
        attended.append((summed[at : at + size] / column).astype(BF16))
    attended = jnp.concatenate(attended, axis=0)
    along, part = out_ref.shape[0], out_ref.shape[1] // 4
    for y in range(along):
        for far in range(2):
            for other in range(2):
                at = ((other * 2 + far) * along + y) * part
                to = (other * 2 + far) * part
                out_ref[y, to : to + part] = attended[at : at + part]


def divide(partial, along):
    rows = partial.shape[1] - TAIL
    return pl.pallas_call(
        divide_kernel,
        out_shape=jax.ShapeDtypeStruct((along, rows // along, HD), BF16),
        compiler_params=params(8),
    )(partial)


def mix_kernel(y_ref, attended_ref, first_ref, *refs):
    *weight_refs, own_ref, other_ref, first, first_sem = refs
    copy = pltpu.make_async_copy(first_ref, first, first_sem.at[0])
    copy.start()
    attended = jnp.concatenate([attended_ref[y_ref[0] ^ i] for i in (0, 1, 3, 2)], axis=1)
    half, width = own_ref.shape
    step = width // 4
    copy.wait()
    for at in range(0, width, step):
        weight = [ref[:, at : at + step] for ref in (first, *weight_refs)]
        weight = jnp.concatenate(weight, axis=0)
        mixed = jnp.dot(attended, weight, preferred_element_type=F32)
        own_ref[:, at : at + step] = mixed[:half]
        other_ref[:, at : at + step] = mixed[half:].astype(BF16)


def mix(y, attended, weights):
    rows = attended.shape[1]
    depth, width = weights[0].shape
    vmem = pl.BlockSpec(memory_space=pltpu.VMEM)
    return pl.pallas_call(
        mix_kernel,
        in_specs=[
            pl.BlockSpec(memory_space=pltpu.SMEM),
            vmem,
            pl.BlockSpec(memory_space=pltpu.HBM),
        ]
        + [vmem] * (len(weights) - 1),
        out_shape=[
            jax.ShapeDtypeStruct((rows // 2, width), F32),
            jax.ShapeDtypeStruct((rows // 2, width), BF16),
        ],
        scratch_shapes=[pltpu.VMEM((depth, width), BF16), pltpu.SemaphoreType.DMA((1,))],
        compiler_params=params(16),
        cost_estimate=pl.CostEstimate(
            flops=8 * rows * width * depth,
            bytes_accessed=8 * width * depth,
            transcendentals=0,
        ),
    )(y, attended, *weights)


def local(tokens, mod_shift, mod_scale, qkv_weight, q_gain, k_gain, out_weight, out_gate):
    rows, width = tokens.shape

    def along_y(block, distance):
        return lax.ppermute(block, "y", [(i, i ^ distance) for i in range(4)])

    def spread(modulated):
        return lax.all_gather(modulated, "y", axis=0, tiled=True)

    far = trade_halves(tokens)
    near, rows_held = modulate_near(tokens, [mod_shift, mod_scale, q_gain, k_gain])
    far, gains = modulate_far(far, rows_held)
    own = jnp.concatenate([spread(near), spread(far)], axis=0)
    queries, keyval = project([own, swap(own, "core")], gains, qkv_weight, 8)
    out_weight, keyval = lax.optimization_barrier((out_weight, keyval))
    half = out_weight.shape[0] // 2
    weights = [along_y(out_weight, i) for i in (1, 3)]
    weights += [along_y(out_weight[:half], 2), along_y(out_weight[half:], 2)]
    queries = lax.all_to_all(queries, NEAR, 0, 0)
    one, two = swap(keyval, "za"), swap(keyval, "zb")
    three = swap(one, "zb")
    partial = attend(queries, jnp.concatenate([keyval, one, two, three], axis=0))
    partial, *weights[:3] = lax.optimization_barrier((partial, *weights[:3]))
    partial = lax.all_to_all(partial, NEAR, 0, 0)
    attended = lax.all_to_all(divide(partial, 4), "y", 0, 0)
    y = lax.axis_index("y").astype(jnp.int32).reshape(1)
    own, other = mix(y, attended, [out_weight, *weights])
    summed = own + swap(other, "core").astype(F32)
    arrived = trade_halves(summed[rows:].astype(BF16)).astype(F32)
    return ((summed[:rows] + arrived) * out_gate).astype(BF16)


def solution(mesh):
    fine = Mesh(mesh.devices.reshape(tuple(AXES.values())), ALL)
    heads = ("y", "zh", "core")
    return jax.shard_map(
        local,
        mesh=fine,
        in_specs=(
            P(ALL, None),
            P(),
            P(),
            P(None, None, heads),
            P(),
            P(),
            P(heads, None),
            P(),
        ),
        out_specs=P(ALL, None),
        check_vma=False,
    )
```
